256 devices in a mesh: dp: 32 (over x, z), seq: 8 (over y, core).
Axes of the slice: x: 4, y: 4, z: 8, core: 2. Of those that a mesh axis runs over, the one named last changes fastest.
Arguments:
- enc_rows: bfloat16 [128, 512, 1280], P('dp', 'seq'), may hold values from -100 to 100
- out_weight: bfloat16 [1280, 512], replicated, may hold values from -3 to 3
- labels: int32 [128, 127], P('dp'), may hold values from 1 to 511
- label_count: int32 [128], P('dp'), may hold values from 1 to 127, as said below
- frame_count: int32 [128], P('dp'), may hold values from 256 to 512, as said below
Outputs:
- logit_grad: bfloat16 [128, 512, 512], P('dp', 'seq')
- row_grad: bfloat16 [128, 512, 1280], P('dp', 'seq')
- weight_grad: float32 [1280, 512], P('dp', 'seq')
The draws below stay inside these ranges and needn't reach their ends.
Inputs may be any that keep to these rules, and one draw needn't show every extreme that they name: `labels`: character ids; id 0 is the blank and never appears. `label_count`: some utterance has 127 labels in every draw. `frame_count`: some utterance has 512 frames in every draw.
All inputs are finite; a program needn't handle non-finite values.
Results may differ from the reference program's by a relative error of at most 0.0043.
Values sent between devices are 32-bit elements; how exact they have to be, the bound alone decides.
No kernel may reach another device: no remote copies, remote signals or barrier semaphores. Data moves between devices by JAX's collectives and lax.ppermute only.
A program may use at most 64 MiB of HBM per device.

```python
import math
import jax
import jax.numpy as jnp
from jax import lax

D = 1280
V = 512
SEQS = 4
FRAMES = 512
L = 127
BATCH = 128
N_DP = 32


def weight_table(key):
    spread = 3.0 / math.sqrt(D)
    drawn = jax.random.normal(jax.random.fold_in(key, 11), (D, V), jnp.float32) * spread
    return jnp.clip(drawn, -3.0, 3.0)


def draw_out_weight(key, part):
    return weight_table(key).astype(jnp.bfloat16)


def draw_enc_rows(key, part):
    base_rows = jnp.clip(jax.random.normal(jax.random.fold_in(key, 21), (BATCH, FRAMES, D), jnp.float32), -6.0, 6.0)
    return jnp.clip(base_rows, -100.0, 100.0).astype(jnp.bfloat16)


def forced_most(key, lowest, highest):
    drawn = jax.random.randint(jax.random.fold_in(key, 31), (BATCH,), lowest, highest + 1)
    forced_spot = jax.random.randint(jax.random.fold_in(key, 32), (), 0, BATCH)
    return jnp.where(jnp.arange(BATCH) == forced_spot, highest, drawn).astype(jnp.int32)


def draw_frame_count(key, part):
    return forced_most(jax.random.fold_in(key, 51), FRAMES // 2, FRAMES)


def draw_label_count(key, part):
    return forced_most(jax.random.fold_in(key, 41), 1, L)


def place_ends(values, own_key, smallest, top_value):
    longest = values.shape.index(max(values.shape))
    spots = []
    for shift in (0, 1):
        where = [jax.random.randint(jax.random.fold_in(own_key, axis), (), 0, length) for axis, length in enumerate(values.shape)]
        where[longest] = (where[longest] + shift) % values.shape[longest]
        spots.append(tuple(where))
    return values.at[spots[0]].set(smallest).at[spots[1]].set(top_value)


def setup_inputs(seed: int = 0) -> dict:
    streams_of = jax.random.split(jax.random.key(seed), 6)
    return {
        "enc_rows": draw_enc_rows(jax.random.fold_in(streams_of[5], 71), 0),
        "out_weight": draw_out_weight(jax.random.fold_in(streams_of[5], 71), 0),
        "labels": place_ends(jax.random.randint(streams_of[2], (BATCH, L), 1, V), jax.random.fold_in(streams_of[2], 1), 1, V - 1).astype(jnp.int32),
        "label_count": draw_label_count(jax.random.fold_in(streams_of[5], 71), 0),
        "frame_count": draw_frame_count(jax.random.fold_in(streams_of[5], 71), 0),
    }


negative_fill = -1.0e30


def merge_three(first_term, second_term, third_term):
    highest = jnp.maximum(jnp.maximum(first_term, second_term), third_term)
    return highest + jnp.log(jnp.exp(first_term - highest) + jnp.exp(second_term - highest) + jnp.exp(third_term - highest))


def shift_right(values, amount):
    filler = jnp.full((values.shape[0], amount), negative_fill, jnp.float32)
    return jnp.concatenate([filler, values[:, :-amount]], axis=1)


def shift_left(values, amount):
    filler = jnp.full((values.shape[0], amount), negative_fill, jnp.float32)
    return jnp.concatenate([values[:, amount:], filler], axis=1)


def advance(current, emission, usable, allowed):
    from_one = shift_right(current, 1)
    from_two = jnp.where(allowed, shift_right(current, 2), negative_fill)
    fresh = merge_three(current, from_one, from_two) + emission
    return jnp.where(usable[:, None], fresh, current)


def retreat(current, emission, usable, allowed_next):
    summed = current + emission
    next_one = shift_left(summed, 1)
    next_two = jnp.where(allowed_next, shift_left(summed, 2), negative_fill)
    fresh = merge_three(summed, next_one, next_two)
    return jnp.where(usable[:, None], fresh, current)


def lattice(labels, label_count):
    utterances, length = labels.shape
    states_wide = 2 * length + 2
    blanks = jnp.zeros((utterances, length + 1), jnp.int32)
    chars = jnp.concatenate([labels, jnp.full((utterances, 1), -1, jnp.int32)], axis=1)
    extended = jnp.stack([blanks, chars], axis=2).reshape(utterances, states_wide)
    earlier = jnp.concatenate([jnp.full((utterances, 2), -2, jnp.int32), extended[:, :-2]], axis=1)
    positions = jnp.arange(states_wide, dtype=jnp.int32)[None, :]
    allowed = (positions % 2 == 1) & (positions >= 3) & (extended != earlier)
    allowed_next = jnp.concatenate([allowed[:, 2:], jnp.zeros((utterances, 2), jnp.bool_)], axis=1)
    zeros_row = jnp.zeros((utterances, states_wide), jnp.float32)
    initial = jnp.where(positions == 0, zeros_row, negative_fill)
    doubled = 2 * label_count[:, None]
    closing = jnp.where((positions == doubled) | (positions == doubled - 1), zeros_row, negative_fill)
    return allowed, allowed_next, initial, closing


def emissions(logprob, labels):
    utterances, frames, vocabulary = logprob.shape
    length = labels.shape[1]
    char_index = jnp.concatenate([jnp.zeros((utterances, 1), jnp.int32), labels], axis=1)
    picked = jnp.take_along_axis(logprob, jnp.broadcast_to(char_index[:, None, :], (utterances, frames, length + 1)), axis=2)
    blank_part = jnp.broadcast_to(picked[:, :, :1], picked.shape)
    label_part = jnp.concatenate([picked[:, :, 1:], jnp.full((utterances, frames, 1), negative_fill, jnp.float32)], axis=2)
    emission = jnp.stack([blank_part, label_part], axis=3).reshape(utterances, frames, 2 * length + 2)
    return jnp.swapaxes(emission, 0, 1), char_index


def forward_pass(initial, emission, usable, allowed):
    def frame_step(current, inputs):
        fresh = advance(current, inputs[0], inputs[1], allowed)
        return fresh, fresh
    return lax.scan(frame_step, initial, (emission, usable))


def backward_pass(closing, emission, usable, allowed_next):
    def frame_step(current, inputs):
        return retreat(current, inputs[0], inputs[1], allowed_next), current
    return lax.scan(frame_step, closing, (emission, usable), reverse=True)


def gradients(logprob, forward_states, backward_states, usable, char_index):
    frames, utterances, states_wide = forward_states.shape
    summed = forward_states + backward_states
    highest = jnp.max(summed, axis=2, keepdims=True)
    log_total = highest + jnp.log(jnp.sum(jnp.exp(summed - highest), axis=2, keepdims=True))
    posterior = jnp.exp(summed - log_total) * usable[:, :, None].astype(jnp.float32)
    paired = posterior.reshape(frames, utterances, states_wide // 2, 2)
    blank_mass = jnp.sum(paired[:, :, :, 0], axis=2, keepdims=True)
    occupancy = jnp.concatenate([blank_mass, paired[:, :, :-1, 1]], axis=2)
    vocabulary = logprob.shape[2]
    one_hot = (char_index[:, :, None] == jnp.arange(vocabulary, dtype=jnp.int32)[None, None, :]).astype(jnp.float32)
    char_mass = jnp.einsum("fup,upv->ufv", occupancy, one_hot, precision=lax.Precision.HIGHEST)
    keep = jnp.swapaxes(usable, 0, 1)[:, :, None].astype(jnp.float32)
    return ((jnp.exp(logprob) - char_mass) * keep).astype(jnp.bfloat16)


def reference(enc_rows, out_weight, labels, label_count, frame_count):
    def one_block(inputs):
        block_rows, block_labels, block_lcount, block_fcount = inputs
        utterances, frames, width_rows = block_rows.shape
        flat_rows = block_rows.reshape(utterances * frames, width_rows)
        logits = jnp.dot(flat_rows, out_weight, preferred_element_type=jnp.float32).reshape(utterances, frames, -1)
        logprob = jax.nn.log_softmax(logits, axis=-1)
        emission, char_index = emissions(logprob, block_labels)
        allowed, allowed_next, initial, closing = lattice(block_labels, block_lcount)
        usable = jnp.arange(frames, dtype=jnp.int32)[:, None] < block_fcount[None, :]
        forward_states = forward_pass(initial, emission, usable, allowed)[1]
        backward_states = backward_pass(closing, emission, usable, allowed_next)[1]
        logit_grad = gradients(logprob, forward_states, backward_states, usable, char_index)
        flat_grad = logit_grad.reshape(utterances * frames, -1)
        row_grad = lax.dot_general(flat_grad, out_weight, (((1,), (1,)), ((), ())), preferred_element_type=jnp.float32)
        row_grad = row_grad.astype(jnp.bfloat16).reshape(utterances, frames, width_rows)
        weight_term = lax.dot_general(flat_rows, flat_grad, (((0,), (0,)), ((), ())), preferred_element_type=jnp.float32)
        return logit_grad, row_grad, weight_term

    blocks = (enc_rows.reshape(N_DP, SEQS, FRAMES, D), labels.reshape(N_DP, SEQS, L),
              label_count.reshape(N_DP, SEQS), frame_count.reshape(N_DP, SEQS))
    logit_grad, row_grad, weight_terms = lax.map(one_block, blocks)
    weight_grad = jnp.sum(weight_terms, axis=0) / BATCH
    return logit_grad.reshape(BATCH, FRAMES, V), row_grad.reshape(BATCH, FRAMES, D), weight_grad
```

```python
import functools

import jax
import jax.numpy as jnp
from jax import lax
from jax.experimental import pallas as pl
from jax.experimental.pallas import tpu as pltpu
from jax.sharding import PartitionSpec as P

negative_fill = -1e30
log2_e = 1.4426950408889634
unroll_steps = 16


def one_hot_of(chars, vocabulary):
    rows = lax.broadcasted_iota(jnp.int32, (vocabulary, chars.shape[1]), 0)
    return jnp.where(rows == chars, 1.0, 0.0).astype(jnp.bfloat16)


def split_parts(values, count):
    parts = []
    for _ in range(count):
        part = values.astype(jnp.bfloat16)
        parts.append(part)
        values = values - part.astype(jnp.float32)
    return parts


def front_kernel(chars_ref, enc_ref, weight_ref, picked_ref, softmax_ref):
    utterances = chars_ref.shape[0]
    rows, vocabulary = softmax_ref.shape
    frames = rows // utterances
    for u in range(utterances):
        span = pl.ds(u * frames, frames)
        logits = jnp.dot(enc_ref[span, :], weight_ref[...], preferred_element_type=jnp.float32)
        highest = jnp.max(logits, axis=1, keepdims=True)
        shifted = logits - highest
        powers = jnp.exp(shifted)
        total = jnp.sum(powers, axis=1, keepdims=True)
        softmax_ref[span, :] = powers / total
        logprob = (shifted - jnp.log(total)) * log2_e
        one_hot = one_hot_of(chars_ref[pl.ds(u, 1), :], vocabulary)
        picked = jnp.zeros((frames, one_hot.shape[1]), jnp.float32)
        for part in reversed(split_parts(logprob, 3)):
            picked = picked + jnp.dot(part, one_hot, preferred_element_type=jnp.float32)
        picked_ref[pl.ds(u, frames, stride=utterances), :] = picked


def lattice_kernel(
    place_ref, counts_ref, *refs, utterances, frames, pieces, vocabulary
):
    piece_refs = refs[:pieces]
    (chars_ref, softmax_ref, enc_ref, grad_ref, keep_ref, send_ref,
     emission, fwd_store, bwd_store, product) = refs[pieces:]
    place = place_ref[0]
    block = frames * utterances
    all_frames = frames * pieces
    rows = 2 * utterances
    lanes = 128

    emission[pl.ds(0, 8), :] = jnp.zeros((8, lanes), jnp.float32)
    emission[pl.ds(8 + block * pieces, 8), :] = jnp.zeros((8, lanes), jnp.float32)
    for k in range(pieces):
        origin = lax.bitwise_xor(place, jnp.int32(k))
        emission[pl.ds(pl.multiple_of(8 + origin * block, 8), block), :] = piece_refs[k][...]

    row = lax.broadcasted_iota(jnp.int32, (rows, lanes), 0)
    lane = lax.broadcasted_iota(jnp.int32, (rows, lanes), 1)
    is_forward = row < utterances
    is_filler = lane == lanes - 1

    chars = chars_ref[...]
    chars_eight = jnp.concatenate([chars, chars], axis=0)
    previous = pltpu.roll(chars_eight, 1, 1)
    following = pltpu.roll(chars_eight, lanes - 1, 1)
    neighbour = jnp.where(is_forward, previous, following)
    barred = (chars_eight == neighbour) | (is_forward & (lane == 0))
    penalty = jnp.where(barred, negative_fill, 0.0)

    last_label = jnp.zeros((rows, lanes), jnp.int32)
    threshold = jnp.full((rows, lanes), -1, jnp.int32)
    for u in range(utterances):
        last_label = jnp.where(row == utterances + u, counts_ref[0, u] - 1, last_label)
        threshold = jnp.where(row == utterances + u, all_frames - counts_ref[1, u], threshold)
    closing = jnp.where(lane == last_label, 0.0, negative_fill)
    start_blank = jnp.where(is_forward & (lane == 0), 0.0, negative_fill)
    start_label = jnp.full((rows, lanes), negative_fill, jnp.float32)
    ones = jnp.ones((rows, lanes), jnp.float32)

    def turned(values):
        return jnp.where(is_forward, pltpu.roll(values, 1, 1), pltpu.roll(values, lanes - 1, 1))

    def chunk_step(chunk, carry):
        label_top, blank_top, label_sum, blank_sum = carry
        label_top = label_top + jnp.log(label_sum) * log2_e
        blank_top = blank_top + jnp.log(blank_sum) * log2_e
        fwd_slot = jnp.where(chunk == place, 0, 1)
        bwd_slot = jnp.where(pieces - 1 - chunk == place, 0, 1)

        def group_step(group, carry):
            label_top, blank_top, label_sum, blank_sum = carry
            first = group * unroll_steps
            base = chunk * frames + first
            fwd_at = pl.multiple_of(8 + utterances * base, 8)
            bwd_at = pl.multiple_of(utterances * (all_frames - base) - utterances * unroll_steps, 8)
            for r in range(unroll_steps):
                ahead = emission[pl.ds(fwd_at + utterances * r, 8), :]
                behind = emission[pl.ds(bwd_at + utterances * (unroll_steps - r), 8), :]
                both = jnp.where(is_forward, ahead, behind)
                blank_emission = jnp.broadcast_to(both[:, lanes - 1 :], (rows, lanes))
                label_emission = jnp.where(is_filler, negative_fill, both)
                going = (base + r) > threshold

                turned_top = turned(label_top)
                turned_sum = turned(label_sum)
                jump_top = turned_top + penalty
                blank_high = jnp.maximum(blank_top, turned_top)
                label_high = jnp.maximum(jnp.maximum(label_top, blank_top), jump_top)
                blank_new = blank_sum * jnp.exp2(blank_top - blank_high) + turned_sum * jnp.exp2(
                    turned_top - blank_high
                )
                label_new = (
                    label_sum * jnp.exp2(label_top - label_high)
                    + blank_sum * jnp.exp2(blank_top - label_high)
                    + turned_sum * jnp.exp2(jump_top - label_high)
                )
                blank_high = jnp.where(going, blank_high, closing)
                label_high = jnp.where(going, label_high, closing)
                blank_sum = jnp.where(going, blank_new, ones)
                label_sum = jnp.where(going, label_new, ones)
                fwd_row = pl.ds(pl.multiple_of((first + r) * rows, rows), rows)
                bwd_row = pl.ds(pl.multiple_of((frames - 1 - first - r) * rows, rows), rows)
                for n, values in enumerate((label_high, blank_high, label_sum, blank_sum)):
                    fwd_store[n, fwd_slot, fwd_row, :] = values
                    bwd_store[n, bwd_slot, bwd_row, :] = values
                label_top = label_high + label_emission
                blank_top = blank_high + blank_emission
            return (label_top, blank_top, label_sum, blank_sum)

        return lax.fori_loop(
            0, frames // unroll_steps, group_step, (label_top, blank_top, ones, ones)
        )

    lax.fori_loop(0, pieces, chunk_step, (start_label, start_blank, ones, ones))

    wide_lane = lax.broadcasted_iota(jnp.int32, (frames, lanes), 1)
    wide_filler = wide_lane == lanes - 1
    frame_index = place * frames + lax.broadcasted_iota(jnp.int32, (frames, 1), 0)
    for u in range(utterances):
        fwd_rows = pl.ds(u, frames, stride=rows)
        bwd_rows = pl.ds(utterances + u, frames, stride=rows)
        local = emission[pl.ds(8 + place * block + u, frames, stride=utterances), :]
        blank_emission = jnp.broadcast_to(local[:, lanes - 1 :], (frames, lanes))
        label_joint = (
            fwd_store[0, 0, fwd_rows, :]
            + jnp.where(wide_filler, negative_fill, local)
            + bwd_store[0, 0, bwd_rows, :]
            + (jnp.log(fwd_store[2, 0, fwd_rows, :]) + jnp.log(bwd_store[2, 0, bwd_rows, :])) * log2_e
        )
        bwd_blank = bwd_store[1, 0, bwd_rows, :] + jnp.log(bwd_store[3, 0, bwd_rows, :]) * log2_e
        blank_joint = (
            fwd_store[1, 0, fwd_rows, :]
            + jnp.log(fwd_store[3, 0, fwd_rows, :]) * log2_e
            + blank_emission
            + pltpu.roll(bwd_blank, 1, 1)
        )
        highest = jnp.max(jnp.maximum(label_joint, blank_joint), axis=1, keepdims=True)
        label_mass = jnp.exp2(label_joint - highest)
        blank_mass = jnp.exp2(blank_joint - highest)
        blank_total = jnp.sum(blank_mass, axis=1, keepdims=True)
        total = jnp.sum(label_mass, axis=1, keepdims=True) + blank_total
        occupancy = jnp.where(wide_filler, blank_total, label_mass) / total
        one_hot = one_hot_of(chars_ref[pl.ds(u, 1), :], vocabulary)
        char_mass = jnp.zeros((frames, vocabulary), jnp.float32)
        for part in reversed(split_parts(occupancy, 3)):
            char_mass = char_mass + lax.dot_general(
                part, one_hot, (((1,), (1,)), ((), ())), preferred_element_type=jnp.float32
            )
        span = pl.ds(u * frames, frames)
        grad = softmax_ref[span, :] - char_mass
        grad = jnp.where(frame_index < counts_ref[1, u], grad, 0.0)
        grad_ref[span, :] = grad.astype(jnp.bfloat16)

    depth = enc_ref.shape[1]
    product[...] = lax.dot_general(
        enc_ref[...], grad_ref[...], (((0,), (0,)), ((), ())), preferred_element_type=jnp.float32
    )
    core = lax.rem(place, 2)
    half = 40
    narrow_low = lax.broadcasted_iota(jnp.int32, (half, lanes), 1) < lanes // 2

    def cut_step(pair, carry):
        upper_at = pl.multiple_of(pair * 2 * half, 8)
        lower_at = pl.multiple_of(pair * 2 * half + half, 8)
        out_at = pl.ds(pl.multiple_of(pair * half, 8), half)
        for y in range(vocabulary // lanes):
            columns = pl.ds(y * lanes, lanes)
            upper = product[pl.ds(upper_at, half), columns] * (1.0 / 128)
            lower = product[pl.ds(lower_at, half), columns] * (1.0 / 128)
            even = jnp.where(narrow_low, upper, pltpu.roll(lower, lanes // 2, 1))
            odd = jnp.where(narrow_low, pltpu.roll(upper, lanes // 2, 1), lower)
            keep_ref[y, out_at, :] = jnp.where(core == 0, even, odd)
            send_ref[y, out_at, :] = jnp.where(core == 0, odd, even)
        return carry

    lax.fori_loop(0, depth // (2 * half), cut_step, 0)


def partner(values, axis, mask):
    size = lax.axis_size(axis)
    return lax.ppermute(values, axis, [(i, i ^ mask) for i in range(size)])


def shards(enc_rows, out_weight, labels, label_count, frame_count):
    utterances, frames, depth = enc_rows.shape
    vocabulary = out_weight.shape[1]
    pieces = lax.axis_size("seq")
    place = lax.axis_index("seq")
    group = lax.axis_index("dp")
    rows = utterances * frames
    lanes = 128
    flat_rows = enc_rows.reshape(rows, depth)
    chars = jnp.pad(labels, ((0, 0), (0, 1)))
    vmem = pl.BlockSpec(memory_space=pltpu.VMEM)
    smem = pl.BlockSpec(memory_space=pltpu.SMEM)

    picked, softmax = pl.pallas_call(
        front_kernel,
        out_shape=(
            jax.ShapeDtypeStruct((rows, lanes), jnp.float32),
            jax.ShapeDtypeStruct((rows, vocabulary), jnp.float32),
        ),
        in_specs=[vmem] * 3,
        out_specs=(vmem, vmem),
        compiler_params=pltpu.CompilerParams(vmem_limit_bytes=32 * 2**20),
    )(chars, flat_rows, out_weight)

    gathered = [picked] + [partner(picked, "seq", k) for k in range(1, pieces)]

    counts = jnp.stack([label_count, frame_count])
    logit_grad, keep, send = pl.pallas_call(
        functools.partial(
            lattice_kernel,
            utterances=utterances,
            frames=frames,
            pieces=pieces,
            vocabulary=vocabulary,
        ),
        out_shape=(
            jax.ShapeDtypeStruct((rows, vocabulary), jnp.bfloat16),
            jax.ShapeDtypeStruct((4, depth // 2, lanes), jnp.float32),
            jax.ShapeDtypeStruct((4, depth // 2, lanes), jnp.float32),
        ),
        in_specs=[smem, smem] + [vmem] * (pieces + 3),
        out_specs=(vmem, vmem, vmem),
        scratch_shapes=[
            pltpu.VMEM((16 + rows * pieces, lanes), jnp.float32),
            pltpu.VMEM((4, 2, 2 * rows, lanes), jnp.float32),
            pltpu.VMEM((4, 2, 2 * rows, lanes), jnp.float32),
            pltpu.VMEM((depth, vocabulary), jnp.float32),
        ],
        compiler_params=pltpu.CompilerParams(vmem_limit_bytes=48 * 2**20),
    )(place.reshape(1), counts, *gathered, chars, softmax, flat_rows)

    row_grad = lax.dot_general(
        logit_grad, out_weight, (((1,), (1,)), ((), ())), preferred_element_type=jnp.float32
    )
    row_grad = row_grad.astype(jnp.bfloat16).reshape(utterances, frames, depth)

    place_y, place_x, place_z = place // 2, group // 8, group % 8
    summed = keep + partner(send, "seq", 1)

    def piece_of(array, index):
        return lax.dynamic_index_in_dim(array, index, 0, keepdims=False)

    total = piece_of(summed, place_y)
    for k in (1, 2, 3):
        total = total + partner(piece_of(summed, place_y ^ k), "seq", 2 * k)
    cut = total.reshape(4, depth // 8, lanes)
    total = piece_of(cut, place_x)
    for k in (1, 2, 3):
        total = total + partner(piece_of(cut, place_x ^ k), "dp", 8 * k)
    cut = jnp.repeat(total.reshape(4, depth // 32, lanes), 2, axis=0)
    along_z = [[x * 8 + z for z in range(8)] for x in range(4)]
    arrived = lax.all_to_all(cut, "dp", 0, 0, axis_index_groups=along_z)
    total = jnp.sum(arrived, axis=0)
    weight_grad = jnp.where(place_z % 2 == 0, total[:, : lanes // 2], total[:, lanes // 2 :])
    return (logit_grad.reshape(utterances, frames, vocabulary), row_grad, weight_grad)


def solution(mesh):
    placed = (P("dp", "seq", None), P(), P("dp", None), P("dp"), P("dp"))
    return jax.shard_map(
        shards,
        mesh=mesh,
        in_specs=placed,
        out_specs=(P("dp", "seq", None), P("dp", "seq", None), P("dp", "seq")),
        check_vma=False,
    )
```

```python
import functools

import jax
import jax.numpy as jnp
from jax import lax
from jax.experimental import pallas as pl
from jax.experimental.pallas import tpu as pltpu
from jax.sharding import PartitionSpec as P

negative_fill = -1e30
log2_e = 1.4426950408889634
unroll_steps = 16
reach = 8
held_chunks = 5


def one_hot_of(chars, vocabulary):
    rows = lax.broadcasted_iota(jnp.int32, (vocabulary, chars.shape[1]), 0)
    return jnp.where(rows == chars, 1.0, 0.0).astype(jnp.bfloat16)


def split_parts(values, count):
    parts = []
    for _ in range(count):
        part = values.astype(jnp.bfloat16)
        parts.append(part)
        values = values - part.astype(jnp.float32)
    return parts


def chars_of(labels_ref):
    blank = jnp.zeros((labels_ref.shape[0], 1), jnp.int32)
    return jnp.concatenate([labels_ref[...], blank], axis=1)


def front_kernel(labels_ref, enc_ref, weight_ref, picked_ref, softmax_ref):
    utterances = labels_ref.shape[0]
    chars = chars_of(labels_ref)
    rows, vocabulary = softmax_ref.shape
    frames = rows // utterances
    for u in range(utterances):
        span = pl.ds(u * frames, frames)
        logits = jnp.dot(enc_ref[span, :], weight_ref[...], preferred_element_type=jnp.float32)
        highest = jnp.max(logits, axis=1, keepdims=True)
        shifted = logits - highest
        powers = jnp.exp(shifted)
        total = jnp.sum(powers, axis=1, keepdims=True)
        softmax_ref[span, :] = powers / total
        logprob = (shifted - jnp.log(total)) * log2_e
        one_hot = one_hot_of(chars[u : u + 1, :], vocabulary)
        picked = jnp.zeros((frames, one_hot.shape[1]), jnp.float32)
        for part in reversed(split_parts(logprob, 3)):
            picked = picked + jnp.dot(part, one_hot, preferred_element_type=jnp.float32)
        picked_ref[pl.ds(u, frames, stride=utterances), :] = picked


def lattice_kernel(
    place_ref, counts_ref, *refs, utterances, frames, pieces, vocabulary
):
    gathered_refs = refs[:2]
    (labels_ref, softmax_ref, enc_ref, grad_ref, keep_ref, send_ref,
     emission, mixed, fixed, fwd_store, bwd_store, product) = refs[2:]
    place, place_x, place_z = place_ref[0], place_ref[1], place_ref[2]
    block = frames * utterances
    all_frames = frames * pieces
    rows = 2 * utterances
    lanes = 128

    emission[pl.ds(0, 8), :] = jnp.zeros((8, lanes), jnp.float32)
    emission[pl.ds(8 + block * pieces, 8), :] = jnp.zeros((8, lanes), jnp.float32)
    for k in range(pieces):
        origin = lax.bitwise_xor(place, jnp.int32(k))
        source = gathered_refs[k % 2]
        emission[pl.ds(pl.multiple_of(8 + origin * block, 8), block), :] = source[
            pl.ds(k // 2 * block, block), :
        ]

    row = lax.broadcasted_iota(jnp.int32, (rows, lanes), 0)
    lane = lax.broadcasted_iota(jnp.int32, (rows, lanes), 1)
    is_forward = row < utterances
    is_filler = lane == lanes - 1
    mirror = jnp.where(is_filler, lanes - 1, lanes - 2 - lane)

    def mirrored(values):
        return jnp.take_along_axis(values, mirror, axis=1)

    def mix_step(chunk, carry):
        base = chunk * frames
        fwd_at = pl.multiple_of(8 + utterances * base, 8)
        bwd_at = pl.multiple_of(utterances * (all_frames - base) - utterances * frames, 8)
        out_at = pl.multiple_of(base * rows, 8)
        for r in range(frames):
            ahead = emission[pl.ds(fwd_at + utterances * r, 8), :]
            behind = emission[pl.ds(bwd_at + utterances * (frames - r), 8), :]
            mixed[pl.ds(out_at + r * rows, rows), :] = jnp.where(is_forward, ahead, mirrored(behind))
        return carry

    lax.fori_loop(0, pieces, mix_step, 0)

    chars = chars_of(labels_ref)
    chars_eight = jnp.concatenate([chars, chars], axis=0)
    chars_eight = jnp.where(is_forward, chars_eight, mirrored(chars_eight))
    barred = (chars_eight == pltpu.roll(chars_eight, 1, 1)) | (lane == 0)
    penalty = jnp.where(barred, negative_fill, 0.0)

    first_lane = jnp.full((rows, lanes), -1, jnp.int32)
    threshold = jnp.full((rows, lanes), -1, jnp.int32)
    for u in range(utterances):
        first_lane = jnp.where(row == utterances + u, lanes - 1 - counts_ref[0, u], first_lane)
        threshold = jnp.where(row == utterances + u, all_frames - counts_ref[1, u], threshold)
    closing = jnp.where(lane == first_lane, 0.0, negative_fill)
    start_blank = jnp.where(is_forward & (lane == 0), 0.0, negative_fill)
    start_label = jnp.full((rows, lanes), negative_fill, jnp.float32)
    ones = jnp.ones((rows, lanes), jnp.float32)
    for k in range(reach):
        fixed[0, k] = pltpu.roll(penalty, k, 1) if k else penalty
        fixed[1, k] = pltpu.roll(closing, k, 1) if k else closing

    def copies(values, count):
        return [values] + [pltpu.roll(values, k, 1) for k in range(1, count)]

    def chunk_step(chunk, carry, held):
        label_top, blank_top, label_sum, blank_sum = carry
        label_top = label_top + jnp.log(label_sum) * log2_e
        blank_top = blank_top + jnp.log(blank_sum) * log2_e
        fwd_slot = jnp.where(chunk == place, 0, 1)
        bwd_slot = jnp.where(pieces - 1 - chunk == place, 0, 1)

        def group_step(group, carry):
            first = group * unroll_steps
            base = chunk * frames + first
            mixed_at = pl.multiple_of(base * rows, rows)
            for r in range(unroll_steps):
                if r % reach == 0:
                    label_tops = copies(carry[0], reach + 1)
                    blank_tops = copies(carry[1], reach)
                    label_sums = copies(carry[2], reach + 1)
                    blank_sums = copies(carry[3], reach)
                both = mixed[pl.ds(mixed_at + r * rows, rows), :]
                blank_emission = jnp.broadcast_to(both[:, lanes - 1 :], (rows, lanes))
                label_emission = jnp.where(is_filler, negative_fill, both)
                if held:
                    going = (base + r) > threshold
                for k in range(reach - r % reach):
                    label_top, blank_top = label_tops[k], blank_tops[k]
                    label_sum, blank_sum = label_sums[k], blank_sums[k]
                    moved_top, moved_sum = label_tops[k + 1], label_sums[k + 1]
                    jump_top = moved_top + fixed[0, k]
                    blank_high = jnp.maximum(blank_top, moved_top)
                    label_high = jnp.maximum(jnp.maximum(label_top, blank_top), jump_top)
                    blank_new = blank_sum * jnp.exp2(blank_top - blank_high) + moved_sum * jnp.exp2(
                        moved_top - blank_high
                    )
                    label_new = (
                        label_sum * jnp.exp2(label_top - label_high)
                        + blank_sum * jnp.exp2(blank_top - label_high)
                        + moved_sum * jnp.exp2(jump_top - label_high)
                    )
                    if held:
                        blank_high = jnp.where(going, blank_high, fixed[1, k])
                        label_high = jnp.where(going, label_high, fixed[1, k])
                        blank_new = jnp.where(going, blank_new, ones)
                        label_new = jnp.where(going, label_new, ones)
                    if k == 0:
                        fwd_row = pl.ds(pl.multiple_of((first + r) * rows, rows), rows)
                        bwd_row = pl.ds(pl.multiple_of((frames - 1 - first - r) * rows, rows), rows)
                        for n, values in enumerate((label_high, blank_high, label_new, blank_new)):
                            fwd_store[n, fwd_slot, fwd_row, :] = values
                            bwd_store[n, bwd_slot, bwd_row, :] = values
                    moved_emission = pltpu.roll(label_emission, k, 1) if k else label_emission
                    label_tops[k] = label_high + moved_emission
                    blank_tops[k] = blank_high + blank_emission
                    label_sums[k] = label_new
                    blank_sums[k] = blank_new
                carry = (label_tops[0], blank_tops[0], label_sums[0], blank_sums[0])
            return carry

        return lax.fori_loop(
            0, frames // unroll_steps, group_step, (label_top, blank_top, ones, ones)
        )

    carry = (start_label, start_blank, ones, ones)
    carry = lax.fori_loop(0, held_chunks, functools.partial(chunk_step, held=True), carry)
    lax.fori_loop(held_chunks, pieces, functools.partial(chunk_step, held=False), carry)

    wide_lane = lax.broadcasted_iota(jnp.int32, (frames, lanes), 1)
    wide_filler = wide_lane == lanes - 1
    wide_label_mirror = jnp.where(wide_filler, lanes - 1, lanes - 2 - wide_lane)
    wide_blank_mirror = lanes - 1 - wide_lane
    frame_index = place * frames + lax.broadcasted_iota(jnp.int32, (frames, 1), 0)
    for u in range(utterances):
        fwd_rows = pl.ds(u, frames, stride=rows)
        bwd_rows = pl.ds(utterances + u, frames, stride=rows)
        local = emission[pl.ds(8 + place * block + u, frames, stride=utterances), :]
        blank_emission = jnp.broadcast_to(local[:, lanes - 1 :], (frames, lanes))
        bwd_label = bwd_store[0, 0, bwd_rows, :] + jnp.log(bwd_store[2, 0, bwd_rows, :]) * log2_e
        label_joint = (
            fwd_store[0, 0, fwd_rows, :]
            + jnp.log(fwd_store[2, 0, fwd_rows, :]) * log2_e
            + jnp.where(wide_filler, negative_fill, local)
            + jnp.take_along_axis(bwd_label, wide_label_mirror, axis=1)
        )
        bwd_blank = bwd_store[1, 0, bwd_rows, :] + jnp.log(bwd_store[3, 0, bwd_rows, :]) * log2_e
        blank_joint = (
            fwd_store[1, 0, fwd_rows, :]
            + jnp.log(fwd_store[3, 0, fwd_rows, :]) * log2_e
            + blank_emission
            + jnp.take_along_axis(bwd_blank, wide_blank_mirror, axis=1)
        )
        highest = jnp.max(jnp.maximum(label_joint, blank_joint), axis=1, keepdims=True)
        label_mass = jnp.exp2(label_joint - highest)
        blank_mass = jnp.exp2(blank_joint - highest)
        blank_total = jnp.sum(blank_mass, axis=1, keepdims=True)
        total = jnp.sum(label_mass, axis=1, keepdims=True) + blank_total
        occupancy = jnp.where(wide_filler, blank_total, label_mass) / total
        one_hot = one_hot_of(chars[u : u + 1, :], vocabulary)
        char_mass = jnp.zeros((frames, vocabulary), jnp.float32)
        for part in reversed(split_parts(occupancy, 3)):
            char_mass = char_mass + lax.dot_general(
                part, one_hot, (((1,), (1,)), ((), ())), preferred_element_type=jnp.float32
            )
        span = pl.ds(u * frames, frames)
        grad = softmax_ref[span, :] - char_mass
        grad = jnp.where(frame_index < counts_ref[1, u], grad, 0.0)
        grad_ref[span, :] = grad.astype(jnp.bfloat16)

    depth = enc_ref.shape[1]
    product[...] = lax.dot_general(
        enc_ref[...], grad_ref[...], (((0,), (0,)), ((), ())), preferred_element_type=jnp.float32
    )
    core, place_y = lax.rem(place, 2), lax.div(place, 2)
    half = 40
    narrow_low = lax.broadcasted_iota(jnp.int32, (half, lanes), 1) < lanes // 2

    def cut_step(pair, carry):
        upper_at = pl.multiple_of(pair * 2 * half, 8)
        lower_at = pl.multiple_of(pair * 2 * half + half, 8)
        far_x = lax.bitwise_xor(lax.div(pair, 4), place_x)
        far_z = lax.bitwise_xor(lax.rem(pair, 4), lax.div(place_z, 2))
        for y in range(vocabulary // lanes):
            columns = pl.ds(y * lanes, lanes)
            far_y = lax.bitwise_xor(jnp.int32(y), place_y)
            upper = product[pl.ds(upper_at, half), columns] * (1.0 / 128)
            lower = product[pl.ds(lower_at, half), columns] * (1.0 / 128)
            even = jnp.where(narrow_low, upper, pltpu.roll(lower, lanes // 2, 1))
            odd = jnp.where(narrow_low, pltpu.roll(upper, lanes // 2, 1), lower)
            even_at = (far_y * 16 + far_x * 4 + far_z) * half
            odd_at = (far_x * 16 + far_y * 4 + far_z) * half
            keep_at = pl.multiple_of(jnp.where(core == 0, even_at, odd_at), 8)
            send_at = pl.multiple_of(jnp.where(core == 0, odd_at, even_at), 8)
            keep_ref[pl.ds(keep_at, half), :] = jnp.where(core == 0, even, odd)
            send_ref[pl.ds(send_at, half), :] = jnp.where(core == 0, odd, even)
        return carry

    lax.fori_loop(0, depth // (2 * half), cut_step, 0)


def partner(values, axis, mask):
    size = lax.axis_size(axis)
    return lax.ppermute(values, axis, [(i, i ^ mask) for i in range(size)])


def crosswise(values, mask, first):
    groups, places = lax.axis_size("dp"), lax.axis_size("seq")
    route = []
    for dp in range(groups):
        for seq in range(places):
            along_y = (seq % 2 == 0) == first
            far = (dp, seq ^ (2 * mask)) if along_y else (dp ^ (8 * mask), seq)
            route.append((dp * places + seq, far[0] * places + far[1]))
    return lax.ppermute(values, ("dp", "seq"), route)


def shards(enc_rows, out_weight, labels, label_count, frame_count):
    utterances, frames, depth = enc_rows.shape
    vocabulary = out_weight.shape[1]
    pieces = lax.axis_size("seq")
    place = lax.axis_index("seq")
    group = lax.axis_index("dp")
    rows = utterances * frames
    lanes = 128
    flat_rows = enc_rows.reshape(rows, depth)
    vmem = pl.BlockSpec(memory_space=pltpu.VMEM)
    smem = pl.BlockSpec(memory_space=pltpu.SMEM)

    picked, softmax = pl.pallas_call(
        front_kernel,
        out_shape=(
            jax.ShapeDtypeStruct((rows, lanes), jnp.float32),
            jax.ShapeDtypeStruct((rows, vocabulary), jnp.float32),
        ),
        in_specs=[vmem] * 3,
        out_specs=(vmem, vmem),
        compiler_params=pltpu.CompilerParams(vmem_limit_bytes=32 * 2**20),
    )(labels, flat_rows, out_weight)

    same_core = jnp.concatenate([picked] + [partner(picked, "seq", k) for k in range(2, pieces, 2)])
    other_core = partner(same_core, "seq", 1)

    counts = jnp.stack([label_count, frame_count])
    places = jnp.stack([place, group // 8, group % 8])
    logit_grad, keep, send = pl.pallas_call(
        functools.partial(
            lattice_kernel,
            utterances=utterances,
            frames=frames,
            pieces=pieces,
            vocabulary=vocabulary,
        ),
        out_shape=(
            jax.ShapeDtypeStruct((rows, vocabulary), jnp.bfloat16),
            jax.ShapeDtypeStruct((2 * depth, lanes), jnp.float32),
            jax.ShapeDtypeStruct((2 * depth, lanes), jnp.float32),
        ),
        in_specs=[smem, smem] + [vmem] * 5,
        out_specs=(vmem, vmem, vmem),
        scratch_shapes=[
            pltpu.VMEM((16 + rows * pieces, lanes), jnp.float32),
            pltpu.VMEM((2 * rows * pieces, lanes), jnp.float32),
            pltpu.VMEM((2, reach, 2 * utterances, lanes), jnp.float32),
            pltpu.VMEM((4, 2, 2 * rows, lanes), jnp.float32),
            pltpu.VMEM((4, 2, 2 * rows, lanes), jnp.float32),
            pltpu.VMEM((depth, vocabulary), jnp.float32),
        ],
        compiler_params=pltpu.CompilerParams(vmem_limit_bytes=48 * 2**20),
    )(places, counts, same_core, other_core, labels, softmax, flat_rows)

    row_grad = lax.dot_general(
        logit_grad, out_weight, (((1,), (1,)), ((), ())), preferred_element_type=jnp.float32
    )
    row_grad = row_grad.astype(jnp.bfloat16).reshape(utterances, frames, depth)

    arrived = partner(send, "seq", 1)
    block = depth // 2
    blocks = [keep[k * block : (k + 1) * block] + arrived[k * block : (k + 1) * block] for k in range(4)]
    total = blocks[0]
    for k in (1, 2, 3):
        total = total + crosswise(blocks[k], k, True)
    block = block // 4
    blocks = [total[k * block : (k + 1) * block] for k in range(4)]
    total = blocks[0]
    for k in (1, 2, 3):
        total = total + crosswise(blocks[k], k, False)
    block = block // 4
    blocks = [total[k * block : (k + 1) * block] for k in range(4)]
    total = blocks[0]
    for k in (1, 2, 3):
        total = total + partner(blocks[k], "dp", 2 * k)
    total = total + partner(total, "dp", 1)
    weight_grad = jnp.where(group % 2 == 0, total[:, : lanes // 2], total[:, lanes // 2 :])
    return (logit_grad.reshape(utterances, frames, vocabulary), row_grad, weight_grad)


def solution(mesh):
    placed = (P("dp", "seq", None), P(), P("dp", None), P("dp"), P("dp"))
    return jax.shard_map(
        shards,
        mesh=mesh,
        in_specs=placed,
        out_specs=(P("dp", "seq", None), P("dp", "seq", None), P("dp", "seq")),
        check_vma=False,
    )
```

```python
import functools

import jax
import jax.numpy as jnp
from jax import lax
from jax.experimental import pallas as pl
from jax.experimental.pallas import tpu as pltpu
from jax.sharding import PartitionSpec as P

negative_fill = -1e30
log2_e = 1.4426950408889634
unroll_steps = 16
loads = 5
reach = 8


def one_hot_of(chars, vocabulary):
    rows = lax.broadcasted_iota(jnp.int32, (vocabulary, chars.shape[1]), 0)
    return jnp.where(rows == chars, 1.0, 0.0).astype(jnp.bfloat16)


def split_parts(values, count):
    parts = []
    for _ in range(count):
        part = values.astype(jnp.bfloat16)
        parts.append(part)
        values = values - part.astype(jnp.float32)
    return parts


def chars_of(labels_ref):
    blank = jnp.zeros((labels_ref.shape[0], 1), jnp.int32)
    return jnp.concatenate([labels_ref[...], blank], axis=1)


def front_kernel(
    labels_ref, enc_ref, weight_ref, picked_ref, softmax_ref, enc_held, weight_held, logits_ref, arrivals
):
    utterances = labels_ref.shape[0]
    rows, vocabulary = softmax_ref.shape
    frames = rows // utterances
    depth = weight_ref.shape[0]
    step = depth // loads
    copies = []
    for n in range(loads):
        part = pl.ds(n * step, step)
        pair = (
            pltpu.make_async_copy(weight_ref.at[part, :], weight_held.at[part, :], arrivals.at[0, n]),
            pltpu.make_async_copy(enc_ref.at[:, part], enc_held.at[:, part], arrivals.at[1, n]),
        )
        for copy in pair:
            copy.start()
        copies.append(pair)
    chars = chars_of(labels_ref)
    one_hots = [one_hot_of(chars[u : u + 1, :], vocabulary) for u in range(utterances)]
    for n in range(loads):
        part = pl.ds(n * step, step)
        for copy in copies[n]:
            copy.wait()
        product = jnp.dot(
            enc_held[:, part], weight_held[part, :], preferred_element_type=jnp.float32
        )
        logits_ref[...] = product if n == 0 else logits_ref[...] + product
    for u in range(utterances):
        span = pl.ds(u * frames, frames)
        logits = logits_ref[span, :]
        highest = jnp.max(logits, axis=1, keepdims=True)
        shifted = logits - highest
        powers = jnp.exp(shifted)
        total = jnp.sum(powers, axis=1, keepdims=True)
        softmax_ref[span, :] = powers / total
        logprob = (shifted - jnp.log(total)) * log2_e
        picked = jnp.zeros((frames, chars.shape[1]), jnp.float32)
        for part in reversed(split_parts(logprob, 3)):
            picked = picked + jnp.dot(part, one_hots[u], preferred_element_type=jnp.float32)
        picked_ref[pl.ds(u, frames, stride=utterances), :] = picked


def merge_two(first_top, first_sum, second_top, second_sum):
    high = jnp.maximum(first_top, second_top)
    return high, first_sum * jnp.exp2(first_top - high) + second_sum * jnp.exp2(second_top - high)


def lattice_kernel(
    place_ref, counts_ref, *refs, utterances, frames, pieces, vocabulary
):
    gathered_refs = refs[:2]
    (labels_ref, softmax_ref, enc_ref, grad_ref, keep_ref, send_ref,
     emission, mixed, fixed, fwd_store, bwd_store, product) = refs[2:]
    place, place_x, place_z = place_ref[0], place_ref[1], place_ref[2]
    block = frames * utterances
    all_frames = frames * pieces
    rows = 2 * utterances
    lanes = 128

    emission[pl.ds(0, 8), :] = jnp.zeros((8, lanes), jnp.float32)
    emission[pl.ds(8 + block * pieces, 8), :] = jnp.zeros((8, lanes), jnp.float32)
    for k in range(pieces):
        chip = lax.rem(lax.div(place, 2) + pieces // 2 - k // 2, pieces // 2)
        origin = 2 * chip + lax.bitwise_xor(lax.rem(place, 2), jnp.int32(k % 2))
        source = gathered_refs[k % 2]
        emission[pl.ds(pl.multiple_of(8 + origin * block, 8), block), :] = source[
            pl.ds(k // 2 * block, block), :
        ]

    row = lax.broadcasted_iota(jnp.int32, (rows, lanes), 0)
    lane = lax.broadcasted_iota(jnp.int32, (rows, lanes), 1)
    is_forward = row < utterances
    is_filler = lane == lanes - 1
    mirror = jnp.where(is_filler, lanes - 1, lanes - 2 - lane)

    def mirrored(values):
        return jnp.take_along_axis(values, mirror, axis=1)

    def mix_step(chunk, carry):
        base = chunk * frames
        fwd_at = pl.multiple_of(8 + utterances * base, 8)
        bwd_at = pl.multiple_of(utterances * (all_frames - base) - utterances * frames, 8)
        out_at = pl.multiple_of(base * rows, 8)
        for r in range(frames):
            ahead = emission[pl.ds(fwd_at + utterances * r, 8), :]
            behind = emission[pl.ds(bwd_at + utterances * (frames - r), 8), :]
            mixed[pl.ds(out_at + r * rows, rows), :] = jnp.where(is_forward, ahead, mirrored(behind))
        return carry

    lax.fori_loop(0, pieces, mix_step, 0)

    chars = chars_of(labels_ref)
    chars_eight = jnp.concatenate([chars, chars], axis=0)
    chars_eight = jnp.where(is_forward, chars_eight, mirrored(chars_eight))
    barred = (chars_eight == pltpu.roll(chars_eight, 1, 1)) | (lane == 0)
    penalty = jnp.where(barred, negative_fill, 0.0)

    first_lane = jnp.full((rows, lanes), -1, jnp.int32)
    threshold = jnp.full((rows, lanes), -1, jnp.int32)
    for u in range(utterances):
        first_lane = jnp.where(row == utterances + u, lanes - 1 - counts_ref[0, u], first_lane)
        threshold = jnp.where(row == utterances + u, all_frames - counts_ref[1, u], threshold)
    closing = jnp.where(lane == first_lane, 0.0, negative_fill)
    start_blank = jnp.where(is_forward & (lane == 0), 0.0, negative_fill)
    start_label = jnp.full((rows, lanes), negative_fill, jnp.float32)
    ones = jnp.ones((rows, lanes), jnp.float32)
    for k in range(reach):
        fixed[0, k] = pltpu.roll(penalty, k, 1) if k else penalty
        fixed[1, k] = pltpu.roll(closing, k, 1) if k else closing

    def copies(values, count):
        return [values] + [pltpu.roll(values, k, 1) for k in range(1, count)]

    def chunk_step(chunk, carry):
        label_top, blank_top, label_sum, blank_sum = carry
        label_top = label_top + jnp.log(label_sum) * log2_e
        blank_top = blank_top + jnp.log(blank_sum) * log2_e
        fwd_slot = jnp.where(chunk == place, 0, 1)
        bwd_slot = jnp.where(pieces - 1 - chunk == place, 0, 1)

        def group_step(group, carry, held):
            first = group * unroll_steps
            base = chunk * frames + first
            mixed_at = pl.multiple_of(base * rows, rows)
            for r in range(unroll_steps):
                if r % reach == 0:
                    label_tops = copies(carry[0], reach + 1)
                    blank_tops = copies(carry[1], reach)
                    label_sums = copies(carry[2], reach + 1)
                    blank_sums = copies(carry[3], reach)
                both = mixed[pl.ds(mixed_at + r * rows, rows), :]
                blank_emission = jnp.broadcast_to(both[:, lanes - 1 :], (rows, lanes))
                label_emission = jnp.where(is_filler, negative_fill, both)
                if held:
                    stays = threshold == base + r
                for k in range(reach - r % reach):
                    label_top, blank_top = label_tops[k], blank_tops[k]
                    label_sum, blank_sum = label_sums[k], blank_sums[k]
                    blank_high, blank_new = merge_two(
                        blank_top, blank_sum, label_tops[k + 1], label_sums[k + 1]
                    )
                    open_jump = fixed[0, k] == 0.0
                    label_high, label_new = merge_two(
                        label_top,
                        label_sum,
                        jnp.where(open_jump, blank_high, blank_top),
                        jnp.where(open_jump, blank_new, blank_sum),
                    )
                    if held:
                        blank_high = jnp.where(stays, fixed[1, k], blank_high)
                        label_high = jnp.where(stays, fixed[1, k], label_high)
                        blank_new = jnp.where(stays, ones, blank_new)
                        label_new = jnp.where(stays, ones, label_new)
                    if k == 0:
                        fwd_row = pl.ds(pl.multiple_of((first + r) * rows, rows), rows)
                        bwd_row = pl.ds(pl.multiple_of((frames - 1 - first - r) * rows, rows), rows)
                        for n, values in enumerate((label_high, blank_high, label_new, blank_new)):
                            fwd_store[n, fwd_slot, fwd_row, :] = values
                            bwd_store[n, bwd_slot, bwd_row, :] = values
                    moved_emission = pltpu.roll(label_emission, k, 1) if k else label_emission
                    label_tops[k] = label_high + moved_emission
                    blank_tops[k] = blank_high + blank_emission
                    label_sums[k] = label_new
                    blank_sums[k] = blank_new
                carry = (label_tops[0], blank_tops[0], label_sums[0], blank_sums[0])
            return carry

        def group_turn(group, carry):
            base = chunk * frames + group * unroll_steps
            begins = functools.reduce(
                jnp.logical_or,
                [
                    (all_frames - counts_ref[1, u] >= base)
                    & (all_frames - counts_ref[1, u] < base + unroll_steps)
                    for u in range(utterances)
                ],
            )
            return lax.cond(
                begins,
                functools.partial(group_step, group, held=True),
                functools.partial(group_step, group, held=False),
                carry,
            )

        return lax.fori_loop(
            0, frames // unroll_steps, group_turn, (label_top, blank_top, ones, ones)
        )

    lax.fori_loop(0, pieces, chunk_step, (start_label, start_blank, ones, ones))

    wide_lane = lax.broadcasted_iota(jnp.int32, (frames, lanes), 1)
    wide_filler = wide_lane == lanes - 1
    wide_label_mirror = jnp.where(wide_filler, lanes - 1, lanes - 2 - wide_lane)
    wide_blank_mirror = lanes - 1 - wide_lane
    frame_index = place * frames + lax.broadcasted_iota(jnp.int32, (frames, 1), 0)
    for u in range(utterances):
        fwd_rows = pl.ds(u, frames, stride=rows)
        bwd_rows = pl.ds(utterances + u, frames, stride=rows)
        local = emission[pl.ds(8 + place * block + u, frames, stride=utterances), :]
        blank_emission = jnp.broadcast_to(local[:, lanes - 1 :], (frames, lanes))
        bwd_label = bwd_store[0, 0, bwd_rows, :] + jnp.log(bwd_store[2, 0, bwd_rows, :]) * log2_e
        label_joint = (
            fwd_store[0, 0, fwd_rows, :]
            + jnp.log(fwd_store[2, 0, fwd_rows, :]) * log2_e
            + jnp.where(wide_filler, negative_fill, local)
            + jnp.take_along_axis(bwd_label, wide_label_mirror, axis=1)
        )
        bwd_blank = bwd_store[1, 0, bwd_rows, :] + jnp.log(bwd_store[3, 0, bwd_rows, :]) * log2_e
        blank_joint = (
            fwd_store[1, 0, fwd_rows, :]
            + jnp.log(fwd_store[3, 0, fwd_rows, :]) * log2_e
            + blank_emission
            + jnp.take_along_axis(bwd_blank, wide_blank_mirror, axis=1)
        )
        highest = jnp.max(jnp.maximum(label_joint, blank_joint), axis=1, keepdims=True)
        label_mass = jnp.exp2(label_joint - highest)
        blank_mass = jnp.exp2(blank_joint - highest)
        blank_total = jnp.sum(blank_mass, axis=1, keepdims=True)
        total = jnp.sum(label_mass, axis=1, keepdims=True) + blank_total
        occupancy = jnp.where(wide_filler, blank_total, label_mass) / total
        one_hot = one_hot_of(chars[u : u + 1, :], vocabulary)
        char_mass = jnp.zeros((frames, vocabulary), jnp.float32)
        for part in reversed(split_parts(occupancy, 3)):
            char_mass = char_mass + lax.dot_general(
                part, one_hot, (((1,), (1,)), ((), ())), preferred_element_type=jnp.float32
            )
        span = pl.ds(u * frames, frames)
        grad = softmax_ref[span, :] - char_mass
        grad = jnp.where(frame_index < counts_ref[1, u], grad, 0.0)
        grad_ref[span, :] = grad.astype(jnp.bfloat16)

    depth = enc_ref.shape[1]
    product[...] = lax.dot_general(
        enc_ref[...], grad_ref[...], (((0,), (0,)), ((), ())), preferred_element_type=jnp.float32
    )
    core, place_y = lax.rem(place, 2), lax.div(place, 2)
    half = 40
    narrow_low = lax.broadcasted_iota(jnp.int32, (half, lanes), 1) < lanes // 2

    def cut_step(pair, carry):
        upper_at = pl.multiple_of(pair * 2 * half, 8)
        lower_at = pl.multiple_of(upper_at + half, 8)
        far_x = lax.rem(lax.div(pair, 4) + 4 - place_x, 4)
        far_z = lax.rem(lax.rem(pair, 4) + 4 - lax.div(place_z, 2), 4)
        for y in range(vocabulary // lanes):
            columns = pl.ds(y * lanes, lanes)
            far_y = lax.rem(y + 4 - place_y, 4)
            upper = product[pl.ds(upper_at, half), columns] * (1.0 / 128)
            lower = product[pl.ds(lower_at, half), columns] * (1.0 / 128)
            even = jnp.where(narrow_low, upper, pltpu.roll(lower, lanes // 2, 1))
            odd = jnp.where(narrow_low, pltpu.roll(upper, lanes // 2, 1), lower)
            even_at = (far_y * 16 + far_x * 4 + far_z) * half
            odd_at = (far_x * 16 + far_y * 4 + far_z) * half
            keep_at = pl.multiple_of(jnp.where(core == 0, even_at, odd_at), 8)
            send_at = pl.multiple_of(jnp.where(core == 0, odd_at, even_at), 8)
            keep_ref[pl.ds(keep_at, half), :] = jnp.where(core == 0, even, odd)
            send_ref[pl.ds(send_at, half), :] = jnp.where(core == 0, odd, even)
        return carry

    lax.fori_loop(0, depth // (2 * half), cut_step, 0, unroll=4)


def lattice_call(
    places, counts, same_core, other_core, labels, softmax, flat_rows,
    *, utterances, frames, pieces, vocabulary,
):
    vmem = pl.BlockSpec(memory_space=pltpu.VMEM)
    smem = pl.BlockSpec(memory_space=pltpu.SMEM)
    rows, lanes, depth = utterances * frames, 128, flat_rows.shape[1]
    return pl.pallas_call(
        functools.partial(
            lattice_kernel,
            utterances=utterances,
            frames=frames,
            pieces=pieces,
            vocabulary=vocabulary,
        ),
        out_shape=(
            jax.ShapeDtypeStruct((rows, vocabulary), jnp.bfloat16),
            jax.ShapeDtypeStruct((2 * depth, lanes), jnp.float32),
            jax.ShapeDtypeStruct((2 * depth, lanes), jnp.float32),
        ),
        in_specs=[smem, smem] + [vmem] * 5,
        out_specs=(vmem, vmem, vmem),
        scratch_shapes=[
            pltpu.VMEM((16 + rows * pieces, lanes), jnp.float32),
            pltpu.VMEM((2 * rows * pieces, lanes), jnp.float32),
            pltpu.VMEM((2, reach, 2 * utterances, lanes), jnp.float32),
            pltpu.VMEM((4, 2, 2 * rows, lanes), jnp.float32),
            pltpu.VMEM((4, 2, 2 * rows, lanes), jnp.float32),
            pltpu.VMEM((depth, vocabulary), jnp.float32),
        ],
        compiler_params=pltpu.CompilerParams(vmem_limit_bytes=48 * 2**20),
    )(places, counts, same_core, other_core, labels, softmax, flat_rows)


def partner(values, axis, mask):
    size = lax.axis_size(axis)
    return lax.ppermute(values, axis, [(i, i ^ mask) for i in range(size)])


def along_y(values, steps):
    places = lax.axis_size("seq")
    return lax.ppermute(values, "seq", [(i, (i + 2 * steps) % places) for i in range(places)])


def up_z(values, steps):
    groups = lax.axis_size("dp")
    return lax.ppermute(values, "dp", [(i, i // 8 * 8 + (i + steps) % 8) for i in range(groups)])


def crosswise(values, steps, first):
    groups, places = lax.axis_size("dp"), lax.axis_size("seq")
    route = []
    for dp in range(groups):
        for seq in range(places):
            if (seq % 2 == 0) == first:
                far = (dp, (seq + 2 * steps) % places)
            else:
                far = ((dp + 8 * steps) % groups, seq)
            route.append((dp * places + seq, far[0] * places + far[1]))
    return lax.ppermute(values, ("dp", "seq"), route)


def shards(enc_rows, out_weight, labels, label_count, frame_count):
    utterances, frames, depth = enc_rows.shape
    vocabulary = out_weight.shape[1]
    pieces = lax.axis_size("seq")
    place = lax.axis_index("seq")
    group = lax.axis_index("dp")
    rows = utterances * frames
    lanes = 128
    flat_rows = enc_rows.reshape(rows, depth)
    vmem = pl.BlockSpec(memory_space=pltpu.VMEM)
    smem = pl.BlockSpec(memory_space=pltpu.SMEM)

    picked, softmax = pl.pallas_call(
        front_kernel,
        out_shape=(
            jax.ShapeDtypeStruct((rows, lanes), jnp.float32),
            jax.ShapeDtypeStruct((rows, vocabulary), jnp.float32),
        ),
        in_specs=[vmem, pl.BlockSpec(memory_space=pl.ANY), pl.BlockSpec(memory_space=pl.ANY)],
        out_specs=(vmem, vmem),
        scratch_shapes=[
            pltpu.VMEM((rows, depth), jnp.bfloat16),
            pltpu.VMEM((depth, vocabulary), jnp.bfloat16),
            pltpu.VMEM((rows, vocabulary), jnp.float32),
            pltpu.SemaphoreType.DMA((2, loads)),
        ],
        compiler_params=pltpu.CompilerParams(vmem_limit_bytes=60 * 2**20),
    )(labels, flat_rows, out_weight)

    far = along_y(picked, 2)
    same_core = jnp.concatenate([picked, along_y(picked, 1), far, along_y(picked, 3)])
    other_core = partner(same_core, "seq", 1)

    counts = jnp.stack([label_count, frame_count])
    places = jnp.stack([place, group // 8, group % 8])
    logit_grad, keep, send = lattice_call(
        places, counts, same_core, other_core, labels, softmax, flat_rows,
        utterances=utterances, frames=frames, pieces=pieces, vocabulary=vocabulary,
    )

    row_grad = lax.dot_general(
        logit_grad, out_weight, (((1,), (1,)), ((), ())), preferred_element_type=jnp.float32
    )
    row_grad = row_grad.astype(jnp.bfloat16).reshape(utterances, frames, depth)

    arrived = partner(send, "seq", 1)
    block = depth // 2
    blocks = [keep[k * block : (k + 1) * block] + arrived[k * block : (k + 1) * block] for k in range(4)]
    total = blocks[0]
    for k in (1, 2, 3):
        total = total + crosswise(blocks[k], k, True)
    total, row_grad = lax.optimization_barrier((total, row_grad))
    block = block // 4
    blocks = [total[k * block : (k + 1) * block] for k in range(4)]
    total = blocks[0]
    for k in (1, 2, 3):
        total = total + crosswise(blocks[k], k, False)
    block = block // 4
    blocks = [total[k * block : (k + 1) * block] for k in range(4)]
    total = blocks[0]
    for k in (1, 2, 3):
        total = total + up_z(blocks[k], 2 * k)
    total = total + partner(total, "dp", 1)
    weight_grad = jnp.where(group % 2 == 0, total[:, : lanes // 2], total[:, lanes // 2 :])
    return (logit_grad.reshape(utterances, frames, vocabulary), row_grad, weight_grad)


def solution(mesh):
    placed = (P("dp", "seq", None), P(), P("dp", None), P("dp"), P("dp"))
    return jax.shard_map(
        shards,
        mesh=mesh,
        in_specs=placed,
        out_specs=(P("dp", "seq", None), P("dp", "seq", None), P("dp", "seq")),
        check_vma=False,
    )
```

```python
import functools

import jax
import jax.numpy as jnp
from jax import lax
from jax.experimental import pallas as pl
from jax.experimental.pallas import tpu as pltpu
from jax.sharding import PartitionSpec as P

negative_fill = -1e30
log2_e = 1.4426950408889634
unroll_steps = 32
loads = 5
reach = 8


def one_hot_of(chars, vocabulary):
    rows = lax.broadcasted_iota(jnp.int32, (vocabulary, chars.shape[1]), 0)
    return jnp.where(rows == chars, 1.0, 0.0).astype(jnp.bfloat16)


def split_parts(values, count):
    parts = []
    for _ in range(count):
        part = values.astype(jnp.bfloat16)
        parts.append(part)
        values = values - part.astype(jnp.float32)
    return parts


def chars_of(labels_ref):
    blank = jnp.zeros((labels_ref.shape[0], 1), jnp.int32)
    return jnp.concatenate([labels_ref[...], blank], axis=1)


def front_kernel(
    labels_ref, enc_ref, weight_ref, picked_ref, softmax_ref, enc_held, weight_held, logits_ref, arrivals
):
    utterances = labels_ref.shape[0]
    rows, vocabulary = softmax_ref.shape
    frames = rows // utterances
    depth = weight_ref.shape[0]
    step = depth // loads
    copies = []
    for n in range(loads):
        part = pl.ds(n * step, step)
        pair = (
            pltpu.make_async_copy(weight_ref.at[part, :], weight_held.at[part, :], arrivals.at[0, n]),
            pltpu.make_async_copy(enc_ref.at[:, part], enc_held.at[:, part], arrivals.at[1, n]),
        )
        for copy in pair:
            copy.start()
        copies.append(pair)
    chars = chars_of(labels_ref)
    one_hots = [one_hot_of(chars[u : u + 1, :], vocabulary) for u in range(utterances)]
    for n in range(loads):
        part = pl.ds(n * step, step)
        for copy in copies[n]:
            copy.wait()
        product = jnp.dot(
            enc_held[:, part], weight_held[part, :], preferred_element_type=jnp.float32
        )
        logits_ref[...] = product if n == 0 else logits_ref[...] + product
    for u in range(utterances):
        span = pl.ds(u * frames, frames)
        logits = logits_ref[span, :]
        highest = jnp.max(logits, axis=1, keepdims=True)
        shifted = logits - highest
        powers = jnp.exp(shifted)
        total = jnp.sum(powers, axis=1, keepdims=True)
        softmax_ref[span, :] = powers / total
        logprob = (shifted - jnp.log(total)) * log2_e
        picked = jnp.zeros((frames, chars.shape[1]), jnp.float32)
        for part in reversed(split_parts(logprob, 3)):
            picked = picked + jnp.dot(part, one_hots[u], preferred_element_type=jnp.float32)
        picked_ref[pl.ds(u, frames, stride=utterances), :] = picked


def merge_two(first_top, first_sum, second_top, second_sum):
    high = jnp.maximum(first_top, second_top)
    return high, first_sum * jnp.exp2(first_top - high) + second_sum * jnp.exp2(second_top - high)


def lattice_kernel(
    place_ref, counts_ref, *refs, utterances, frames, pieces, vocabulary
):
    gathered_refs = refs[:2]
    labels_ref, softmax_ref, enc_ref, grad_ref = refs[2:6]
    keep_refs, send_refs = refs[6:10], refs[10:14]
    emission, mixed, fixed, fwd_store, bwd_store, product = refs[14:]
    place, place_x, place_z = place_ref[0], place_ref[1], place_ref[2]
    block = frames * utterances
    all_frames = frames * pieces
    rows = 2 * utterances
    lanes = 128

    emission[pl.ds(0, 8), :] = jnp.zeros((8, lanes), jnp.float32)
    emission[pl.ds(8 + block * pieces, 8), :] = jnp.zeros((8, lanes), jnp.float32)
    for k in range(pieces):
        chip = lax.rem(lax.div(place, 2) + pieces // 2 - k // 2, pieces // 2)
        origin = 2 * chip + lax.bitwise_xor(lax.rem(place, 2), jnp.int32(k % 2))
        source = gathered_refs[k % 2]
        emission[pl.ds(pl.multiple_of(8 + origin * block, 8), block), :] = source[
            pl.ds(k // 2 * block, block), :
        ]

    row = lax.broadcasted_iota(jnp.int32, (rows, lanes), 0)
    lane = lax.broadcasted_iota(jnp.int32, (rows, lanes), 1)
    is_forward = row < utterances
    is_filler = lane == lanes - 1
    mirror = jnp.where(is_filler, lanes - 1, lanes - 2 - lane)

    def mirrored(values):
        return jnp.take_along_axis(values, mirror, axis=1)

    def mix_step(chunk, carry):
        base = chunk * frames
        fwd_at = pl.multiple_of(8 + utterances * base, 8)
        bwd_at = pl.multiple_of(utterances * (all_frames - base) - utterances * frames, 8)
        out_at = pl.multiple_of(base * rows, 8)
        for r in range(frames):
            ahead = emission[pl.ds(fwd_at + utterances * r, 8), :]
            behind = emission[pl.ds(bwd_at + utterances * (frames - r), 8), :]
            mixed[pl.ds(out_at + r * rows, rows), :] = jnp.where(is_forward, ahead, mirrored(behind))
        return carry

    lax.fori_loop(0, pieces, mix_step, 0)

    chars = chars_of(labels_ref)
    chars_eight = jnp.concatenate([chars, chars], axis=0)
    chars_eight = jnp.where(is_forward, chars_eight, mirrored(chars_eight))
    barred = (chars_eight == pltpu.roll(chars_eight, 1, 1)) | (lane == 0)
    penalty = jnp.where(barred, negative_fill, 0.0)

    first_lane = jnp.full((rows, lanes), -1, jnp.int32)
    threshold = jnp.full((rows, lanes), -1, jnp.int32)
    for u in range(utterances):
        first_lane = jnp.where(row == utterances + u, lanes - 1 - counts_ref[0, u], first_lane)
        threshold = jnp.where(row == utterances + u, all_frames - counts_ref[1, u], threshold)
    closing = jnp.where(lane == first_lane, 0.0, negative_fill)
    start_blank = jnp.where(is_forward & (lane == 0), 0.0, negative_fill)
    start_label = jnp.full((rows, lanes), negative_fill, jnp.float32)
    ones = jnp.ones((rows, lanes), jnp.float32)
    for k in range(reach):
        fixed[0, k] = pltpu.roll(penalty, k, 1) if k else penalty
        fixed[1, k] = pltpu.roll(closing, k, 1) if k else closing

    def copies(values, count):
        return [values] + [pltpu.roll(values, k, 1) for k in range(1, count)]

    def chunk_step(chunk, carry):
        label_top, blank_top, label_sum, blank_sum = carry
        label_top = label_top + jnp.log(label_sum) * log2_e
        blank_top = blank_top + jnp.log(blank_sum) * log2_e
        fwd_slot = jnp.where(chunk == place, 0, 1)
        bwd_slot = jnp.where(pieces - 1 - chunk == place, 0, 1)

        def group_step(group, carry, held):
            first = group * unroll_steps
            base = chunk * frames + first
            mixed_at = pl.multiple_of(base * rows, rows)
            for r in range(unroll_steps):
                if r % reach == 0:
                    label_tops = copies(carry[0], reach + 1)
                    blank_tops = copies(carry[1], reach)
                    label_sums = copies(carry[2], reach + 1)
                    blank_sums = copies(carry[3], reach)
                both = mixed[pl.ds(mixed_at + r * rows, rows), :]
                blank_emission = jnp.broadcast_to(both[:, lanes - 1 :], (rows, lanes))
                label_emission = jnp.where(is_filler, negative_fill, both)
                if held:
                    stays = threshold == base + r
                for k in range(reach - r % reach):
                    label_top, blank_top = label_tops[k], blank_tops[k]
                    label_sum, blank_sum = label_sums[k], blank_sums[k]
                    blank_high, blank_new = merge_two(
                        blank_top, blank_sum, label_tops[k + 1], label_sums[k + 1]
                    )
                    open_jump = fixed[0, k] == 0.0
                    label_high, label_new = merge_two(
                        label_top,
                        label_sum,
                        jnp.where(open_jump, blank_high, blank_top),
                        jnp.where(open_jump, blank_new, blank_sum),
                    )
                    if held:
                        blank_high = jnp.where(stays, fixed[1, k], blank_high)
                        label_high = jnp.where(stays, fixed[1, k], label_high)
                        blank_new = jnp.where(stays, ones, blank_new)
                        label_new = jnp.where(stays, ones, label_new)
                    if k == 0:
                        fwd_row = pl.ds(pl.multiple_of((first + r) * rows, rows), rows)
                        bwd_row = pl.ds(pl.multiple_of((frames - 1 - first - r) * rows, rows), rows)
                        for n, values in enumerate((label_high, blank_high, label_new, blank_new)):
                            fwd_store[n, fwd_slot, fwd_row, :] = values
                            bwd_store[n, bwd_slot, bwd_row, :] = values
                    moved_emission = pltpu.roll(label_emission, k, 1) if k else label_emission
                    label_tops[k] = label_high + moved_emission
                    blank_tops[k] = blank_high + blank_emission
                    label_sums[k] = label_new
                    blank_sums[k] = blank_new
                carry = (label_tops[0], blank_tops[0], label_sums[0], blank_sums[0])
            return carry

        def group_turn(group, carry):
            base = chunk * frames + group * unroll_steps
            begins = functools.reduce(
                jnp.logical_or,
                [
                    (all_frames - counts_ref[1, u] >= base)
                    & (all_frames - counts_ref[1, u] < base + unroll_steps)
                    for u in range(utterances)
                ],
            )
            return lax.cond(
                begins,
                functools.partial(group_step, group, held=True),
                functools.partial(group_step, group, held=False),
                carry,
            )

        return lax.fori_loop(
            0, frames // unroll_steps, group_turn, (label_top, blank_top, ones, ones)
        )

    lax.fori_loop(0, pieces, chunk_step, (start_label, start_blank, ones, ones))

    wide_lane = lax.broadcasted_iota(jnp.int32, (frames, lanes), 1)
    wide_filler = wide_lane == lanes - 1
    wide_label_mirror = jnp.where(wide_filler, lanes - 1, lanes - 2 - wide_lane)
    wide_blank_mirror = lanes - 1 - wide_lane
    frame_index = place * frames + lax.broadcasted_iota(jnp.int32, (frames, 1), 0)
    for u in range(utterances):
        fwd_rows = pl.ds(u, frames, stride=rows)
        bwd_rows = pl.ds(utterances + u, frames, stride=rows)
        local = emission[pl.ds(8 + place * block + u, frames, stride=utterances), :]
        blank_emission = jnp.broadcast_to(local[:, lanes - 1 :], (frames, lanes))
        bwd_label = bwd_store[0, 0, bwd_rows, :] + jnp.log(bwd_store[2, 0, bwd_rows, :]) * log2_e
        label_joint = (
            fwd_store[0, 0, fwd_rows, :]
            + jnp.log(fwd_store[2, 0, fwd_rows, :]) * log2_e
            + jnp.where(wide_filler, negative_fill, local)
            + jnp.take_along_axis(bwd_label, wide_label_mirror, axis=1)
        )
        bwd_blank = bwd_store[1, 0, bwd_rows, :] + jnp.log(bwd_store[3, 0, bwd_rows, :]) * log2_e
        blank_joint = (
            fwd_store[1, 0, fwd_rows, :]
            + jnp.log(fwd_store[3, 0, fwd_rows, :]) * log2_e
            + blank_emission
            + jnp.take_along_axis(bwd_blank, wide_blank_mirror, axis=1)
        )
        highest = jnp.max(jnp.maximum(label_joint, blank_joint), axis=1, keepdims=True)
        label_mass = jnp.exp2(label_joint - highest)
        blank_mass = jnp.exp2(blank_joint - highest)
        blank_total = jnp.sum(blank_mass, axis=1, keepdims=True)
        total = jnp.sum(label_mass, axis=1, keepdims=True) + blank_total
        occupancy = jnp.where(wide_filler, blank_total, label_mass) / total
        one_hot = one_hot_of(chars[u : u + 1, :], vocabulary)
        char_mass = jnp.zeros((frames, vocabulary), jnp.float32)
        for part in reversed(split_parts(occupancy, 3)):
            char_mass = char_mass + lax.dot_general(
                part, one_hot, (((1,), (1,)), ((), ())), preferred_element_type=jnp.float32
            )
        span = pl.ds(u * frames, frames)
        grad = softmax_ref[span, :] - char_mass
        grad = jnp.where(frame_index < counts_ref[1, u], grad, 0.0)
        grad_ref[span, :] = grad.astype(jnp.bfloat16)

    depth = enc_ref.shape[1]
    product[...] = lax.dot_general(
        enc_ref[...], grad_ref[...], (((0,), (0,)), ((), ())), preferred_element_type=jnp.float32
    )
    core, place_y = lax.rem(place, 2), lax.div(place, 2)
    half = 40
    narrow_low = lax.broadcasted_iota(jnp.int32, (half, lanes), 1) < lanes // 2

    def cut(target, to_first, steps):
        straight = narrow_low == to_first
        for near in range(4):
            y = lax.rem(place_y + jnp.where(to_first, steps, near), 4)
            x = lax.rem(place_x + jnp.where(to_first, near, steps), 4)
            columns = pl.ds(pl.multiple_of(y * lanes, lanes), lanes)
            for far_z in range(4):
                z = lax.rem(lax.div(place_z, 2) + far_z, 4)
                even_at = (x * 4 + z) * 2 * half
                straight_at = pl.multiple_of(even_at + jnp.where(to_first, 0, half), 8)
                moved_at = pl.multiple_of(even_at + jnp.where(to_first, half, 0), 8)
                moved = pltpu.roll(product[pl.ds(moved_at, half), columns], lanes // 2, 1)
                target[pl.ds((near * 4 + far_z) * half, half), :] = jnp.where(
                    straight, product[pl.ds(straight_at, half), columns], moved
                ) * (1.0 / 128)

    for steps in range(4):
        cut(send_refs[steps], core == 1, steps)
        cut(keep_refs[steps], core == 0, steps)


def lattice_call(
    places, counts, same_core, other_core, labels, softmax, flat_rows,
    *, utterances, frames, pieces, vocabulary,
):
    vmem = pl.BlockSpec(memory_space=pltpu.VMEM)
    smem = pl.BlockSpec(memory_space=pltpu.SMEM)
    rows, lanes, depth = utterances * frames, 128, flat_rows.shape[1]
    return pl.pallas_call(
        functools.partial(
            lattice_kernel,
            utterances=utterances,
            frames=frames,
            pieces=pieces,
            vocabulary=vocabulary,
        ),
        out_shape=(
            jax.ShapeDtypeStruct((rows, vocabulary), jnp.bfloat16),
            *[jax.ShapeDtypeStruct((depth // 2, lanes), jnp.float32)] * 8,
        ),
        in_specs=[smem, smem] + [vmem] * 5,
        out_specs=(vmem,) * 9,
        scratch_shapes=[
            pltpu.VMEM((16 + rows * pieces, lanes), jnp.float32),
            pltpu.VMEM((2 * rows * pieces, lanes), jnp.float32),
            pltpu.VMEM((2, reach, 2 * utterances, lanes), jnp.float32),
            pltpu.VMEM((4, 2, 2 * rows, lanes), jnp.float32),
            pltpu.VMEM((4, 2, 2 * rows, lanes), jnp.float32),
            pltpu.VMEM((depth, vocabulary), jnp.float32),
        ],
        compiler_params=pltpu.CompilerParams(vmem_limit_bytes=48 * 2**20),
    )(places, counts, same_core, other_core, labels, softmax, flat_rows)


def partner(values, axis, mask):
    size = lax.axis_size(axis)
    return lax.ppermute(values, axis, [(i, i ^ mask) for i in range(size)])


def along_y(values, steps):
    places = lax.axis_size("seq")
    return lax.ppermute(values, "seq", [(i, (i + 2 * steps) % places) for i in range(places)])


def up_z(values, steps):
    groups = lax.axis_size("dp")
    return lax.ppermute(values, "dp", [(i, i // 8 * 8 + (i + steps) % 8) for i in range(groups)])


def crosswise(values, steps, first):
    groups, places = lax.axis_size("dp"), lax.axis_size("seq")
    route = []
    for dp in range(groups):
        for seq in range(places):
            if (seq % 2 == 0) == first:
                far = (dp, (seq + 2 * steps) % places)
            else:
                far = ((dp + 8 * steps) % groups, seq)
            route.append((dp * places + seq, far[0] * places + far[1]))
    return lax.ppermute(values, ("dp", "seq"), route)


def shards(enc_rows, out_weight, labels, label_count, frame_count):
    utterances, frames, depth = enc_rows.shape
    vocabulary = out_weight.shape[1]
    pieces = lax.axis_size("seq")
    place = lax.axis_index("seq")
    group = lax.axis_index("dp")
    rows = utterances * frames
    lanes = 128
    flat_rows = enc_rows.reshape(rows, depth)
    vmem = pl.BlockSpec(memory_space=pltpu.VMEM)
    smem = pl.BlockSpec(memory_space=pltpu.SMEM)

    picked, softmax = pl.pallas_call(
        front_kernel,
        out_shape=(
            jax.ShapeDtypeStruct((rows, lanes), jnp.float32),
            jax.ShapeDtypeStruct((rows, vocabulary), jnp.float32),
        ),
        in_specs=[vmem, pl.BlockSpec(memory_space=pl.ANY), pl.BlockSpec(memory_space=pl.ANY)],
        out_specs=(vmem, vmem),
        scratch_shapes=[
            pltpu.VMEM((rows, depth), jnp.bfloat16),
            pltpu.VMEM((depth, vocabulary), jnp.bfloat16),
            pltpu.VMEM((rows, vocabulary), jnp.float32),
            pltpu.SemaphoreType.DMA((2, loads)),
        ],
        compiler_params=pltpu.CompilerParams(vmem_limit_bytes=60 * 2**20),
    )(labels, flat_rows, out_weight)

    same_core = jnp.concatenate([picked] + [along_y(picked, k) for k in (1, 2, 3)])
    other_core = partner(same_core, "seq", 1)

    counts = jnp.stack([label_count, frame_count])
    places = jnp.stack([place, group // 8, group % 8])
    logit_grad, *cuts = lattice_call(
        places, counts, same_core, other_core, labels, softmax, flat_rows,
        utterances=utterances, frames=frames, pieces=pieces, vocabulary=vocabulary,
    )

    row_grad = lax.dot_general(
        logit_grad, out_weight, (((1,), (1,)), ((), ())), preferred_element_type=jnp.float32
    )
    row_grad = row_grad.astype(jnp.bfloat16).reshape(utterances, frames, depth)

    keep, send = cuts[:4], cuts[4:]
    block = depth // 2
    blocks = {k: keep[k] + partner(send[k], "seq", 1) for k in (2, 1, 3, 0)}
    total = blocks[0]
    for k in (2, 1, 3):
        total = total + crosswise(blocks[k], k, True)
    total, row_grad = lax.optimization_barrier((total, row_grad))
    block = block // 4
    blocks = [total[k * block : (k + 1) * block] for k in range(4)]
    total = blocks[0]
    for k in (2, 1, 3):
        total = total + crosswise(blocks[k], k, False)
    block = block // 4
    blocks = [total[k * block : (k + 1) * block] for k in range(4)]
    total = blocks[0]
    for k in (2, 1, 3):
        total = total + up_z(blocks[k], 2 * k)
    total = total + partner(total, "dp", 1)
    weight_grad = jnp.where(group % 2 == 0, total[:, : lanes // 2], total[:, lanes // 2 :])
    return (logit_grad.reshape(utterances, frames, vocabulary), row_grad, weight_grad)


def solution(mesh):
    placed = (P("dp", "seq", None), P(), P("dp", None), P("dp"), P("dp"))
    return jax.shard_map(
        shards,
        mesh=mesh,
        in_specs=placed,
        out_specs=(P("dp", "seq", None), P("dp", "seq", None), P("dp", "seq")),
        check_vma=False,
    )
```

```python
import functools

import jax
import jax.numpy as jnp
from jax import lax
from jax.experimental import pallas as pl
from jax.experimental.pallas import tpu as pltpu
from jax.sharding import PartitionSpec as P

negative_fill = -1e30
log2_e = 1.4426950408889634
unroll_steps = 32
loads = 5
reach = 8


def one_hot_of(chars, vocabulary):
    rows = lax.broadcasted_iota(jnp.int32, (vocabulary, chars.shape[1]), 0)
    return jnp.where(rows == chars, 1.0, 0.0).astype(jnp.bfloat16)


def split_parts(values, count):
    parts = []
    for _ in range(count):
        part = values.astype(jnp.bfloat16)
        parts.append(part)
        values = values - part.astype(jnp.float32)
    return parts


def chars_of(labels_ref):
    blank = jnp.zeros((labels_ref.shape[0], 1), jnp.int32)
    return jnp.concatenate([labels_ref[...], blank], axis=1)


def front_kernel(
    labels_ref, enc_ref, weight_ref, picked_ref, softmax_ref, enc_held, weight_held, logits_ref, arrivals
):
    utterances = labels_ref.shape[0]
    rows, vocabulary = softmax_ref.shape
    frames = rows // utterances
    depth = weight_ref.shape[0]
    step = depth // loads
    copies = []
    for n in range(loads):
        part = pl.ds(n * step, step)
        pair = (
            pltpu.make_async_copy(weight_ref.at[part, :], weight_held.at[part, :], arrivals.at[0, n]),
            pltpu.make_async_copy(enc_ref.at[:, part], enc_held.at[:, part], arrivals.at[1, n]),
        )
        for copy in pair:
            copy.start()
        copies.append(pair)
    chars = chars_of(labels_ref)
    one_hots = [one_hot_of(chars[u : u + 1, :], vocabulary) for u in range(utterances)]
    for n in range(loads):
        part = pl.ds(n * step, step)
        for copy in copies[n]:
            copy.wait()
        product = jnp.dot(
            enc_held[:, part], weight_held[part, :], preferred_element_type=jnp.float32
        )
        logits_ref[...] = product if n == 0 else logits_ref[...] + product
    for u in range(utterances):
        span = pl.ds(u * frames, frames)
        logits = logits_ref[span, :]
        highest = jnp.max(logits, axis=1, keepdims=True)
        shifted = logits - highest
        powers = jnp.exp(shifted)
        total = jnp.sum(powers, axis=1, keepdims=True)
        softmax_ref[span, :] = powers / total
        logprob = (shifted - jnp.log(total)) * log2_e
        picked = jnp.zeros((frames, chars.shape[1]), jnp.float32)
        for part in reversed(split_parts(logprob, 3)):
            picked = picked + jnp.dot(part, one_hots[u], preferred_element_type=jnp.float32)
        picked_ref[pl.ds(u, frames, stride=utterances), :] = picked


def merge_two(first_top, first_sum, second_top, second_sum):
    high = jnp.maximum(first_top, second_top)
    return high, first_sum * jnp.exp2(first_top - high) + second_sum * jnp.exp2(second_top - high)


def lattice_kernel(
    place_ref, counts_ref, *refs, utterances, frames, pieces, vocabulary
):
    gathered_refs, refs = refs[:2], refs[2:]
    labels_ref, softmax_ref, enc_ref, grad_ref = refs[:4]
    keep_refs, send_refs = refs[4:8], refs[8:12]
    emission, mixed, fixed, fwd_store, bwd_store, product = refs[12:]
    place, place_x, place_z = place_ref[0], place_ref[1], place_ref[2]
    block = frames * utterances
    all_frames = frames * pieces
    rows = 2 * utterances
    lanes = 128

    emission[pl.ds(0, 8), :] = jnp.zeros((8, lanes), jnp.float32)
    emission[pl.ds(8 + block * pieces, 8), :] = jnp.zeros((8, lanes), jnp.float32)
    for k in range(pieces):
        chip = lax.rem(lax.div(place, 2) + 4 - k // 2, 4)
        origin = 2 * chip + lax.bitwise_xor(lax.rem(place, 2), jnp.int32(k % 2))
        emission[pl.ds(pl.multiple_of(8 + origin * block, 8), block), :] = gathered_refs[k % 2][
            pl.ds(k // 2 * block, block), :
        ]

    row = lax.broadcasted_iota(jnp.int32, (rows, lanes), 0)
    lane = lax.broadcasted_iota(jnp.int32, (rows, lanes), 1)
    is_forward = row < utterances
    is_filler = lane == lanes - 1
    mirror = jnp.where(is_filler, lanes - 1, lanes - 2 - lane)

    def mirrored(values):
        return jnp.take_along_axis(values, mirror, axis=1)

    def mix(base):
        fwd_at = pl.multiple_of(8 + utterances * base, 8)
        bwd_at = pl.multiple_of(utterances * (all_frames - base - unroll_steps), 8)
        out_at = pl.multiple_of(base * rows, rows)
        for r in range(unroll_steps):
            ahead = emission[pl.ds(fwd_at + utterances * r, 8), :]
            behind = emission[pl.ds(bwd_at + utterances * (unroll_steps - r), 8), :]
            mixed[pl.ds(out_at + r * rows, rows), :] = jnp.where(is_forward, ahead, mirrored(behind))

    mix(jnp.int32(0))

    chars = chars_of(labels_ref)
    chars_eight = jnp.concatenate([chars, chars], axis=0)
    chars_eight = jnp.where(is_forward, chars_eight, mirrored(chars_eight))
    barred = (chars_eight == pltpu.roll(chars_eight, 1, 1)) | (lane == 0)
    penalty = jnp.where(barred, negative_fill, 0.0)

    first_lane = jnp.full((rows, lanes), -1, jnp.int32)
    threshold = jnp.full((rows, lanes), -1, jnp.int32)
    for u in range(utterances):
        first_lane = jnp.where(row == utterances + u, lanes - 1 - counts_ref[0, u], first_lane)
        threshold = jnp.where(row == utterances + u, all_frames - counts_ref[1, u], threshold)
    closing = jnp.where(lane == first_lane, 0.0, negative_fill)
    start_blank = jnp.where(is_forward & (lane == 0), 0.0, negative_fill)
    start_label = jnp.full((rows, lanes), negative_fill, jnp.float32)
    ones = jnp.ones((rows, lanes), jnp.float32)
    for k in range(reach):
        fixed[0, k] = pltpu.roll(penalty, k, 1) if k else penalty
        fixed[1, k] = pltpu.roll(closing, k, 1) if k else closing

    def copies(values, count):
        return [values] + [pltpu.roll(values, k, 1) for k in range(1, count)]

    def chunk_step(chunk, carry):
        label_top, blank_top, label_sum, blank_sum = carry
        label_top = label_top + jnp.log(label_sum) * log2_e
        blank_top = blank_top + jnp.log(blank_sum) * log2_e
        fwd_slot = jnp.where(chunk == place, 0, 1)
        bwd_slot = jnp.where(pieces - 1 - chunk == place, 0, 1)

        def group_step(group, carry, held):
            first = group * unroll_steps
            base = chunk * frames + first
            mixed_at = pl.multiple_of(base * rows, rows)
            for r in range(unroll_steps):
                if r % reach == 0:
                    label_tops = copies(carry[0], reach + 1)
                    blank_tops = copies(carry[1], reach)
                    label_sums = copies(carry[2], reach + 1)
                    blank_sums = copies(carry[3], reach)
                both = mixed[pl.ds(mixed_at + r * rows, rows), :]
                blank_emission = jnp.broadcast_to(both[:, lanes - 1 :], (rows, lanes))
                label_emission = jnp.where(is_filler, negative_fill, both)
                if held:
                    stays = threshold == base + r
                for k in range(reach - r % reach):
                    label_top, blank_top = label_tops[k], blank_tops[k]
                    label_sum, blank_sum = label_sums[k], blank_sums[k]
                    blank_high, blank_new = merge_two(
                        blank_top, blank_sum, label_tops[k + 1], label_sums[k + 1]
                    )
                    open_jump = fixed[0, k] == 0.0
                    label_high, label_new = merge_two(
                        label_top,
                        label_sum,
                        jnp.where(open_jump, blank_high, blank_top),
                        jnp.where(open_jump, blank_new, blank_sum),
                    )
                    if held:
                        blank_high = jnp.where(stays, fixed[1, k], blank_high)
                        label_high = jnp.where(stays, fixed[1, k], label_high)
                        blank_new = jnp.where(stays, ones, blank_new)
                        label_new = jnp.where(stays, ones, label_new)
                    if k == 0:
                        fwd_row = pl.ds(pl.multiple_of((first + r) * rows, rows), rows)
                        bwd_row = pl.ds(pl.multiple_of((frames - 1 - first - r) * rows, rows), rows)
                        for n, values in enumerate((label_high, blank_high, label_new, blank_new)):
                            fwd_store[n, fwd_slot, fwd_row, :] = values
                            bwd_store[n, bwd_slot, bwd_row, :] = values
                    moved_emission = pltpu.roll(label_emission, k, 1) if k else label_emission
                    label_tops[k] = label_high + moved_emission
                    blank_tops[k] = blank_high + blank_emission
                    label_sums[k] = label_new
                    blank_sums[k] = blank_new
                carry = (label_tops[0], blank_tops[0], label_sums[0], blank_sums[0])
            mix(jnp.minimum(base + unroll_steps, all_frames - unroll_steps))
            return carry

        def group_turn(group, carry):
            base = chunk * frames + group * unroll_steps
            begins = functools.reduce(
                jnp.logical_or,
                [
                    (all_frames - counts_ref[1, u] >= base)
                    & (all_frames - counts_ref[1, u] < base + unroll_steps)
                    for u in range(utterances)
                ],
            )
            return lax.cond(
                begins,
                functools.partial(group_step, group, held=True),
                functools.partial(group_step, group, held=False),
                carry,
            )

        return lax.fori_loop(
            0, frames // unroll_steps, group_turn, (label_top, blank_top, ones, ones)
        )

    lax.fori_loop(0, pieces, chunk_step, (start_label, start_blank, ones, ones))

    wide_lane = lax.broadcasted_iota(jnp.int32, (frames, lanes), 1)
    wide_filler = wide_lane == lanes - 1
    wide_label_mirror = jnp.where(wide_filler, lanes - 1, lanes - 2 - wide_lane)
    wide_blank_mirror = lanes - 1 - wide_lane
    frame_index = place * frames + lax.broadcasted_iota(jnp.int32, (frames, 1), 0)
    for u in range(utterances):
        fwd_rows = pl.ds(u, frames, stride=rows)
        bwd_rows = pl.ds(utterances + u, frames, stride=rows)
        local = emission[pl.ds(8 + place * block + u, frames, stride=utterances), :]
        blank_emission = jnp.broadcast_to(local[:, lanes - 1 :], (frames, lanes))
        bwd_label = bwd_store[0, 0, bwd_rows, :] + jnp.log(bwd_store[2, 0, bwd_rows, :]) * log2_e
        label_joint = (
            fwd_store[0, 0, fwd_rows, :]
            + jnp.log(fwd_store[2, 0, fwd_rows, :]) * log2_e
            + jnp.where(wide_filler, negative_fill, local)
            + jnp.take_along_axis(bwd_label, wide_label_mirror, axis=1)
        )
        bwd_blank = bwd_store[1, 0, bwd_rows, :] + jnp.log(bwd_store[3, 0, bwd_rows, :]) * log2_e
        blank_joint = (
            fwd_store[1, 0, fwd_rows, :]
            + jnp.log(fwd_store[3, 0, fwd_rows, :]) * log2_e
            + blank_emission
            + jnp.take_along_axis(bwd_blank, wide_blank_mirror, axis=1)
        )
        highest = jnp.max(jnp.maximum(label_joint, blank_joint), axis=1, keepdims=True)
        label_mass = jnp.exp2(label_joint - highest)
        blank_mass = jnp.exp2(blank_joint - highest)
        blank_total = jnp.sum(blank_mass, axis=1, keepdims=True)
        total = jnp.sum(label_mass, axis=1, keepdims=True) + blank_total
        occupancy = jnp.where(wide_filler, blank_total, label_mass) / total
        one_hot = one_hot_of(chars[u : u + 1, :], vocabulary)
        char_mass = jnp.zeros((frames, vocabulary), jnp.float32)
        for part in reversed(split_parts(occupancy, 3)):
            char_mass = char_mass + lax.dot_general(
                part, one_hot, (((1,), (1,)), ((), ())), preferred_element_type=jnp.float32
            )
        span = pl.ds(u * frames, frames)
        grad = softmax_ref[span, :] - char_mass
        grad = jnp.where(frame_index < counts_ref[1, u], grad, 0.0)
        grad_ref[span, :] = grad.astype(jnp.bfloat16)

    depth = enc_ref.shape[1]
    product[...] = lax.dot_general(
        enc_ref[...], grad_ref[...], (((0,), (0,)), ((), ())), preferred_element_type=jnp.float32
    )
    core, place_y = lax.rem(place, 2), lax.div(place, 2)
    half = 40
    narrow_low = lax.broadcasted_iota(jnp.int32, (half, lanes), 1) < lanes // 2

    def cut(target, to_first, steps):
        straight = narrow_low == to_first
        for near in range(4):
            y = lax.rem(place_y + jnp.where(to_first, steps, near), 4)
            x = lax.rem(place_x + jnp.where(to_first, near, steps), 4)
            columns = pl.ds(pl.multiple_of(y * lanes, lanes), lanes)
            for far_z in range(4):
                z = lax.rem(lax.div(place_z, 2) + far_z, 4)
                even_at = (x * 4 + z) * 2 * half
                straight_at = pl.multiple_of(even_at + jnp.where(to_first, 0, half), 8)
                moved_at = pl.multiple_of(even_at + jnp.where(to_first, half, 0), 8)
                moved = pltpu.roll(product[pl.ds(moved_at, half), columns], lanes // 2, 1)
                target[pl.ds((near * 4 + far_z) * half, half), :] = jnp.where(
                    straight, product[pl.ds(straight_at, half), columns], moved
                ) * (1.0 / 128)

    for steps in range(4):
        cut(send_refs[steps], core == 1, steps)
        cut(keep_refs[steps], core == 0, steps)


def lattice_call(
    places, counts, same_core, other_core, labels, softmax, flat_rows,
    *, utterances, frames, pieces, vocabulary,
):
    vmem = pl.BlockSpec(memory_space=pltpu.VMEM)
    smem = pl.BlockSpec(memory_space=pltpu.SMEM)
    rows, lanes, depth = utterances * frames, 128, flat_rows.shape[1]
    return pl.pallas_call(
        functools.partial(
            lattice_kernel,
            utterances=utterances,
            frames=frames,
            pieces=pieces,
            vocabulary=vocabulary,
        ),
        out_shape=(
            jax.ShapeDtypeStruct((rows, vocabulary), jnp.bfloat16),
            *[jax.ShapeDtypeStruct((depth // 2, lanes), jnp.float32)] * 8,
        ),
        in_specs=[smem, smem] + [vmem] * 5,
        out_specs=(vmem,) * 9,
        scratch_shapes=[
            pltpu.VMEM((16 + rows * pieces, lanes), jnp.float32),
            pltpu.VMEM((2 * rows * pieces, lanes), jnp.float32),
            pltpu.VMEM((2, reach, 2 * utterances, lanes), jnp.float32),
            pltpu.VMEM((4, 2, 2 * rows, lanes), jnp.float32),
            pltpu.VMEM((4, 2, 2 * rows, lanes), jnp.float32),
            pltpu.VMEM((depth, vocabulary), jnp.float32),
        ],
        compiler_params=pltpu.CompilerParams(vmem_limit_bytes=48 * 2**20),
    )(places, counts, same_core, other_core, labels, softmax, flat_rows)


def partner(values, axis, mask):
    size = lax.axis_size(axis)
    return lax.ppermute(values, axis, [(i, i ^ mask) for i in range(size)])


def along_y(values, steps):
    places = lax.axis_size("seq")
    return lax.ppermute(values, "seq", [(i, (i + 2 * steps) % places) for i in range(places)])


def up_z(values, steps):
    groups = lax.axis_size("dp")
    return lax.ppermute(values, "dp", [(i, i // 8 * 8 + (i + steps) % 8) for i in range(groups)])


def crosswise(values, steps, first):
    groups, places = lax.axis_size("dp"), lax.axis_size("seq")
    route = []
    for dp in range(groups):
        for seq in range(places):
            if (seq % 2 == 0) == first:
                far = (dp, (seq + 2 * steps) % places)
            else:
                far = ((dp + 8 * steps) % groups, seq)
            route.append((dp * places + seq, far[0] * places + far[1]))
    return lax.ppermute(values, ("dp", "seq"), route)


def shards(enc_rows, out_weight, labels, label_count, frame_count):
    utterances, frames, depth = enc_rows.shape
    vocabulary = out_weight.shape[1]
    pieces = lax.axis_size("seq")
    place = lax.axis_index("seq")
    group = lax.axis_index("dp")
    rows = utterances * frames
    lanes = 128
    flat_rows = enc_rows.reshape(rows, depth)
    vmem = pl.BlockSpec(memory_space=pltpu.VMEM)
    smem = pl.BlockSpec(memory_space=pltpu.SMEM)

    picked, softmax = pl.pallas_call(
        front_kernel,
        out_shape=(
            jax.ShapeDtypeStruct((rows, lanes), jnp.float32),
            jax.ShapeDtypeStruct((rows, vocabulary), jnp.float32),
        ),
        in_specs=[vmem, pl.BlockSpec(memory_space=pl.ANY), pl.BlockSpec(memory_space=pl.ANY)],
        out_specs=(vmem, vmem),
        scratch_shapes=[
            pltpu.VMEM((rows, depth), jnp.bfloat16),
            pltpu.VMEM((depth, vocabulary), jnp.bfloat16),
            pltpu.VMEM((rows, vocabulary), jnp.float32),
            pltpu.SemaphoreType.DMA((2, loads)),
        ],
        compiler_params=pltpu.CompilerParams(vmem_limit_bytes=60 * 2**20),
    )(labels, flat_rows, out_weight)

    same_core = jnp.concatenate([picked] + [along_y(picked, k) for k in (1, 2, 3)])
    other_core = partner(same_core, "seq", 1)

    counts = jnp.stack([label_count, frame_count])
    places = jnp.stack([place, group // 8, group % 8])
    logit_grad, *cuts = lattice_call(
        places, counts, same_core, other_core, labels, softmax, flat_rows,
        utterances=utterances, frames=frames, pieces=pieces, vocabulary=vocabulary,
    )

    row_grad = lax.dot_general(
        logit_grad, out_weight, (((1,), (1,)), ((), ())), preferred_element_type=jnp.float32
    )
    row_grad = row_grad.astype(jnp.bfloat16).reshape(utterances, frames, depth)

    keep, send = cuts[:4], cuts[4:]
    block = depth // 2
    blocks = {k: keep[k] + partner(send[k], "seq", 1) for k in (2, 1, 3, 0)}
    total = blocks[0]
    for k in (2, 1, 3):
        total = total + crosswise(blocks[k], k, True)
    total, row_grad = lax.optimization_barrier((total, row_grad))
    block = block // 4
    blocks = [total[k * block : (k + 1) * block] for k in range(4)]
    total = blocks[0]
    for k in (2, 1, 3):
        total = total + crosswise(blocks[k], k, False)
    block = block // 4
    blocks = [total[k * block : (k + 1) * block] for k in range(4)]
    total = blocks[0]
    for k in (2, 1, 3):
        total = total + up_z(blocks[k], 2 * k)
    total = total + partner(total, "dp", 1)
    weight_grad = jnp.where(group % 2 == 0, total[:, : lanes // 2], total[:, lanes // 2 :])
    return (logit_grad.reshape(utterances, frames, vocabulary), row_grad, weight_grad)


def solution(mesh):
    placed = (P("dp", "seq", None), P(), P("dp", None), P("dp"), P("dp"))
    return jax.shard_map(
        shards,
        mesh=mesh,
        in_specs=placed,
        out_specs=(P("dp", "seq", None), P("dp", "seq", None), P("dp", "seq")),
        check_vma=False,
    )
```

```python
import functools

import jax
import jax.numpy as jnp
from jax import lax
from jax.experimental import pallas as pl
from jax.experimental.pallas import tpu as pltpu
from jax.sharding import PartitionSpec as P

negative_fill = -1e30
log2_e = 1.4426950408889634
unroll_steps = 32
loads = 5
reach = 8


def one_hot_of(chars, vocabulary):
    rows = lax.broadcasted_iota(jnp.int32, (vocabulary, chars.shape[1]), 0)
    return jnp.where(rows == chars, 1.0, 0.0).astype(jnp.bfloat16)


def split_parts(values, count):
    parts = []
    for _ in range(count):
        part = values.astype(jnp.bfloat16)
        parts.append(part)
        values = values - part.astype(jnp.float32)
    return parts


def chars_of(labels_ref):
    blank = jnp.zeros((labels_ref.shape[0], 1), jnp.int32)
    return jnp.concatenate([labels_ref[...], blank], axis=1)


def front_kernel(
    labels_ref, enc_ref, weight_ref, picked_ref, softmax_ref, enc_held, weight_held, logits_ref, arrivals
):
    utterances = labels_ref.shape[0]
    rows, vocabulary = softmax_ref.shape
    frames = rows // utterances
    depth = weight_ref.shape[0]
    step = depth // loads
    copies = []
    for n in range(loads):
        part = pl.ds(n * step, step)
        pair = (
            pltpu.make_async_copy(weight_ref.at[part, :], weight_held.at[part, :], arrivals.at[0, n]),
            pltpu.make_async_copy(enc_ref.at[:, part], enc_held.at[:, part], arrivals.at[1, n]),
        )
        for copy in pair:
            copy.start()
        copies.append(pair)
    chars = chars_of(labels_ref)
    one_hots = [one_hot_of(chars[u : u + 1, :], vocabulary) for u in range(utterances)]
    for n in range(loads):
        part = pl.ds(n * step, step)
        for copy in copies[n]:
            copy.wait()
        product = jnp.dot(
            enc_held[:, part], weight_held[part, :], preferred_element_type=jnp.float32
        )
        logits_ref[...] = product if n == 0 else logits_ref[...] + product
    for u in range(utterances):
        span = pl.ds(u * frames, frames)
        logits = logits_ref[span, :]
        highest = jnp.max(logits, axis=1, keepdims=True)
        shifted = logits - highest
        powers = jnp.exp(shifted)
        total = jnp.sum(powers, axis=1, keepdims=True)
        softmax_ref[span, :] = powers / total
        logprob = (shifted - jnp.log(total)) * log2_e
        picked = jnp.zeros((frames, chars.shape[1]), jnp.float32)
        for part in reversed(split_parts(logprob, 3)):
            picked = picked + jnp.dot(part, one_hots[u], preferred_element_type=jnp.float32)
        picked_ref[pl.ds(u, frames, stride=utterances), :] = picked


def merge_two(first_top, first_sum, second_top, second_sum):
    high = jnp.maximum(first_top, second_top)
    return high, first_sum * jnp.exp2(first_top - high) + second_sum * jnp.exp2(second_top - high)


def lattice_kernel(
    place_ref, counts_ref, *refs, utterances, frames, pieces, vocabulary
):
    gathered_refs, refs = refs[:2], refs[2:]
    labels_ref, softmax_ref, enc_ref, grad_ref = refs[:4]
    keep_refs, send_refs = refs[4:8], refs[8:12]
    emission, mixed, fixed, fwd_store, bwd_store, product = refs[12:]
    place, place_x, place_z = place_ref[0], place_ref[1], place_ref[2]
    block = frames * utterances
    all_frames = frames * pieces
    rows = 2 * utterances
    lanes = 128

    emission[pl.ds(0, 8), :] = jnp.zeros((8, lanes), jnp.float32)
    emission[pl.ds(8 + block * pieces, 8), :] = jnp.zeros((8, lanes), jnp.float32)
    for k in range(pieces):
        chip = lax.rem(lax.div(place, 2) + 4 - k // 2, 4)
        origin = 2 * chip + lax.bitwise_xor(lax.rem(place, 2), jnp.int32(k % 2))
        emission[pl.ds(pl.multiple_of(8 + origin * block, 8), block), :] = gathered_refs[k % 2][
            pl.ds(k // 2 * block, block), :
        ]

    row = lax.broadcasted_iota(jnp.int32, (rows, lanes), 0)
    lane = lax.broadcasted_iota(jnp.int32, (rows, lanes), 1)
    is_forward = row < utterances
    is_filler = lane == lanes - 1
    mirror = jnp.where(is_filler, lanes - 1, lanes - 2 - lane)

    def mirrored(values):
        return jnp.take_along_axis(values, mirror, axis=1)

    def mix(base):
        fwd_at = pl.multiple_of(8 + utterances * base, 8)
        bwd_at = pl.multiple_of(utterances * (all_frames - base - unroll_steps), 8)
        out_at = pl.multiple_of(base * rows, rows)
        for r in range(unroll_steps):
            ahead = emission[pl.ds(fwd_at + utterances * r, 8), :]
            behind = emission[pl.ds(bwd_at + utterances * (unroll_steps - r), 8), :]
            mixed[pl.ds(out_at + r * rows, rows), :] = jnp.where(is_forward, ahead, mirrored(behind))

    mix(jnp.int32(0))

    chars = chars_of(labels_ref)
    chars_eight = jnp.concatenate([chars, chars], axis=0)
    chars_eight = jnp.where(is_forward, chars_eight, mirrored(chars_eight))
    barred = (chars_eight == pltpu.roll(chars_eight, 1, 1)) | (lane == 0)
    penalty = jnp.where(barred, negative_fill, 0.0)

    first_lane = jnp.full((rows, lanes), -1, jnp.int32)
    threshold = jnp.full((rows, lanes), -1, jnp.int32)
    for u in range(utterances):
        first_lane = jnp.where(row == utterances + u, lanes - 1 - counts_ref[0, u], first_lane)
        threshold = jnp.where(row == utterances + u, all_frames - counts_ref[1, u], threshold)
    closing = jnp.where(lane == first_lane, 0.0, negative_fill)
    start_blank = jnp.where(is_forward & (lane == 0), 0.0, negative_fill)
    start_label = jnp.full((rows, lanes), negative_fill, jnp.float32)
    ones = jnp.ones((rows, lanes), jnp.float32)
    for k in range(reach):
        fixed[0, k] = pltpu.roll(penalty, k, 1) if k else penalty
        fixed[1, k] = pltpu.roll(closing, k, 1) if k else closing

    def copies(values, count):
        return [values] + [pltpu.roll(values, k, 1) for k in range(1, count)]

    def chunk_step(chunk, carry):
        label_top, blank_top, label_sum, blank_sum = carry
        label_top = label_top + jnp.log(label_sum) * log2_e
        blank_top = blank_top + jnp.log(blank_sum) * log2_e
        fwd_slot = jnp.where(chunk == place, 0, 1)
        bwd_slot = jnp.where(pieces - 1 - chunk == place, 0, 1)

        def group_step(group, carry, held):
            first = group * unroll_steps
            base = chunk * frames + first
            mixed_at = pl.multiple_of(base * rows, rows)
            for r in range(unroll_steps):
                if r % reach == 0:
                    label_tops = copies(carry[0], reach + 1)
                    blank_tops = copies(carry[1], reach)
                    label_sums = copies(carry[2], reach + 1)
                    blank_sums = copies(carry[3], reach)
                both = mixed[pl.ds(mixed_at + r * rows, rows), :]
                blank_emission = jnp.broadcast_to(both[:, lanes - 1 :], (rows, lanes))
                label_emission = jnp.where(is_filler, negative_fill, both)
                if held:
                    stays = threshold == base + r
                for k in range(reach - r % reach):
                    label_top, blank_top = label_tops[k], blank_tops[k]
                    label_sum, blank_sum = label_sums[k], blank_sums[k]
                    blank_high, blank_new = merge_two(
                        blank_top, blank_sum, label_tops[k + 1], label_sums[k + 1]
                    )
                    open_jump = fixed[0, k] == 0.0
                    label_high, label_new = merge_two(
                        label_top,
                        label_sum,
                        jnp.where(open_jump, blank_high, blank_top),
                        jnp.where(open_jump, blank_new, blank_sum),
                    )
                    if held:
                        blank_high = jnp.where(stays, fixed[1, k], blank_high)
                        label_high = jnp.where(stays, fixed[1, k], label_high)
                        blank_new = jnp.where(stays, ones, blank_new)
                        label_new = jnp.where(stays, ones, label_new)
                    if k == 0:
                        fwd_row = pl.ds(pl.multiple_of((first + r) * rows, rows), rows)
                        bwd_row = pl.ds(pl.multiple_of((frames - 1 - first - r) * rows, rows), rows)
                        for n, values in enumerate((label_high, blank_high, label_new, blank_new)):
                            fwd_store[n, fwd_slot, fwd_row, :] = values
                            bwd_store[n, bwd_slot, bwd_row, :] = values
                    moved_emission = pltpu.roll(label_emission, k, 1) if k else label_emission
                    label_tops[k] = label_high + moved_emission
                    blank_tops[k] = blank_high + blank_emission
                    label_sums[k] = label_new
                    blank_sums[k] = blank_new
                carry = (label_tops[0], blank_tops[0], label_sums[0], blank_sums[0])
            mix(jnp.minimum(base + unroll_steps, all_frames - unroll_steps))
            return carry

        def group_turn(group, carry):
            base = chunk * frames + group * unroll_steps
            begins = functools.reduce(
                jnp.logical_or,
                [
                    (all_frames - counts_ref[1, u] >= base)
                    & (all_frames - counts_ref[1, u] < base + unroll_steps)
                    for u in range(utterances)
                ],
            )
            return lax.cond(
                begins,
                functools.partial(group_step, group, held=True),
                functools.partial(group_step, group, held=False),
                carry,
            )

        return lax.fori_loop(
            0, frames // unroll_steps, group_turn, (label_top, blank_top, ones, ones)
        )

    lax.fori_loop(0, pieces, chunk_step, (start_label, start_blank, ones, ones))

    wide_lane = lax.broadcasted_iota(jnp.int32, (frames, lanes), 1)
    wide_filler = wide_lane == lanes - 1
    wide_label_mirror = jnp.where(wide_filler, lanes - 1, lanes - 2 - wide_lane)
    wide_blank_mirror = lanes - 1 - wide_lane
    frame_index = place * frames + lax.broadcasted_iota(jnp.int32, (frames, 1), 0)
    for u in range(utterances):
        fwd_rows = pl.ds(u, frames, stride=rows)
        bwd_rows = pl.ds(utterances + u, frames, stride=rows)
        local = emission[pl.ds(8 + place * block + u, frames, stride=utterances), :]
        blank_emission = jnp.broadcast_to(local[:, lanes - 1 :], (frames, lanes))
        bwd_label = bwd_store[0, 0, bwd_rows, :] + jnp.log(bwd_store[2, 0, bwd_rows, :]) * log2_e
        label_joint = (
            fwd_store[0, 0, fwd_rows, :]
            + jnp.log(fwd_store[2, 0, fwd_rows, :]) * log2_e
            + jnp.where(wide_filler, negative_fill, local)
            + jnp.take_along_axis(bwd_label, wide_label_mirror, axis=1)
        )
        bwd_blank = bwd_store[1, 0, bwd_rows, :] + jnp.log(bwd_store[3, 0, bwd_rows, :]) * log2_e
        blank_joint = (
            fwd_store[1, 0, fwd_rows, :]
            + jnp.log(fwd_store[3, 0, fwd_rows, :]) * log2_e
            + blank_emission
            + jnp.take_along_axis(bwd_blank, wide_blank_mirror, axis=1)
        )
        highest = jnp.max(jnp.maximum(label_joint, blank_joint), axis=1, keepdims=True)
        label_mass = jnp.exp2(label_joint - highest)
        blank_mass = jnp.exp2(blank_joint - highest)
        blank_total = jnp.sum(blank_mass, axis=1, keepdims=True)
        total = jnp.sum(label_mass, axis=1, keepdims=True) + blank_total
        occupancy = jnp.where(wide_filler, blank_total, label_mass) / total
        one_hot = one_hot_of(chars[u : u + 1, :], vocabulary)
        char_mass = jnp.zeros((frames, vocabulary), jnp.float32)
        for part in reversed(split_parts(occupancy, 3)):
            char_mass = char_mass + lax.dot_general(
                part, one_hot, (((1,), (1,)), ((), ())), preferred_element_type=jnp.float32
            )
        span = pl.ds(u * frames, frames)
        grad = softmax_ref[span, :] - char_mass
        grad = jnp.where(frame_index < counts_ref[1, u], grad, 0.0)
        grad_ref[span, :] = grad.astype(jnp.bfloat16)

    depth = enc_ref.shape[1]
    product[...] = lax.dot_general(
        enc_ref[...], grad_ref[...], (((0,), (0,)), ((), ())), preferred_element_type=jnp.float32
    )
    core, place_y = lax.rem(place, 2), lax.div(place, 2)
    half = 40
    narrow_low = lax.broadcasted_iota(jnp.int32, (half, lanes), 1) < lanes // 2

    def cut(target, to_first, steps):
        straight = narrow_low == to_first
        for near in range(4):
            y = lax.rem(place_y + jnp.where(to_first, steps, near), 4)
            x = lax.rem(place_x + jnp.where(to_first, near, steps), 4)
            columns = pl.ds(pl.multiple_of(y * lanes, lanes), lanes)
            for far_z in range(4):
                z = lax.rem(lax.div(place_z, 2) + far_z, 4)
                even_at = (x * 4 + z) * 2 * half
                straight_at = pl.multiple_of(even_at + jnp.where(to_first, 0, half), 8)
                moved_at = pl.multiple_of(even_at + jnp.where(to_first, half, 0), 8)
                moved = pltpu.roll(product[pl.ds(moved_at, half), columns], lanes // 2, 1)
                target[pl.ds((near * 4 + far_z) * half, half), :] = jnp.where(
                    straight, product[pl.ds(straight_at, half), columns], moved
                ) * (1.0 / 128)

    for steps in range(4):
        cut(send_refs[steps], core == 1, steps)
        cut(keep_refs[steps], core == 0, steps)


def lattice_call(
    places, counts, same_core, other_core, labels, softmax, flat_rows,
    *, utterances, frames, pieces, vocabulary,
):
    vmem = pl.BlockSpec(memory_space=pltpu.VMEM)
    smem = pl.BlockSpec(memory_space=pltpu.SMEM)
    rows, lanes, depth = utterances * frames, 128, flat_rows.shape[1]
    return pl.pallas_call(
        functools.partial(
            lattice_kernel,
            utterances=utterances,
            frames=frames,
            pieces=pieces,
            vocabulary=vocabulary,
        ),
        out_shape=(
            jax.ShapeDtypeStruct((rows, vocabulary), jnp.bfloat16),
            *[jax.ShapeDtypeStruct((depth // 2, lanes), jnp.float32)] * 8,
        ),
        in_specs=[smem, smem] + [vmem] * 5,
        out_specs=(vmem,) * 9,
        scratch_shapes=[
            pltpu.VMEM((16 + rows * pieces, lanes), jnp.float32),
            pltpu.VMEM((2 * rows * pieces, lanes), jnp.float32),
            pltpu.VMEM((2, reach, 2 * utterances, lanes), jnp.float32),
            pltpu.VMEM((4, 2, 2 * rows, lanes), jnp.float32),
            pltpu.VMEM((4, 2, 2 * rows, lanes), jnp.float32),
            pltpu.VMEM((depth, vocabulary), jnp.float32),
        ],
        compiler_params=pltpu.CompilerParams(vmem_limit_bytes=48 * 2**20),
    )(places, counts, same_core, other_core, labels, softmax, flat_rows)


def partner(values, axis, mask):
    size = lax.axis_size(axis)
    return lax.ppermute(values, axis, [(i, i ^ mask) for i in range(size)])


def along_y(values, steps):
    places = lax.axis_size("seq")
    return lax.ppermute(values, "seq", [(i, (i + 2 * steps) % places) for i in range(places)])


def up_z(values, steps):
    groups = lax.axis_size("dp")
    return lax.ppermute(values, "dp", [(i, i // 8 * 8 + (i + steps) % 8) for i in range(groups)])


def crosswise(values, steps, first):
    groups, places = lax.axis_size("dp"), lax.axis_size("seq")
    route = []
    for dp in range(groups):
        for seq in range(places):
            if (seq % 2 == 0) == first:
                far = (dp, (seq + 2 * steps) % places)
            else:
                far = ((dp + 8 * steps) % groups, seq)
            route.append((dp * places + seq, far[0] * places + far[1]))
    return lax.ppermute(values, ("dp", "seq"), route)


def shards(enc_rows, out_weight, labels, label_count, frame_count):
    utterances, frames, depth = enc_rows.shape
    vocabulary = out_weight.shape[1]
    pieces = lax.axis_size("seq")
    place = lax.axis_index("seq")
    group = lax.axis_index("dp")
    rows = utterances * frames
    lanes = 128
    flat_rows = enc_rows.reshape(rows, depth)
    vmem = pl.BlockSpec(memory_space=pltpu.VMEM)
    smem = pl.BlockSpec(memory_space=pltpu.SMEM)

    picked, softmax = pl.pallas_call(
        front_kernel,
        out_shape=(
            jax.ShapeDtypeStruct((rows, lanes), jnp.float32),
            jax.ShapeDtypeStruct((rows, vocabulary), jnp.float32),
        ),
        in_specs=[vmem, pl.BlockSpec(memory_space=pl.ANY), pl.BlockSpec(memory_space=pl.ANY)],
        out_specs=(vmem, vmem),
        scratch_shapes=[
            pltpu.VMEM((rows, depth), jnp.bfloat16),
            pltpu.VMEM((depth, vocabulary), jnp.bfloat16),
            pltpu.VMEM((rows, vocabulary), jnp.float32),
            pltpu.SemaphoreType.DMA((2, loads)),
        ],
        compiler_params=pltpu.CompilerParams(vmem_limit_bytes=60 * 2**20),
    )(labels, flat_rows, out_weight)

    far = along_y(picked, 2)
    same_core = jnp.concatenate([picked, along_y(picked, 1), far, along_y(picked, 3)])
    other_core = partner(same_core, "seq", 1)

    counts = jnp.stack([label_count, frame_count])
    places = jnp.stack([place, group // 8, group % 8])
    logit_grad, *cuts = lattice_call(
        places, counts, same_core, other_core, labels, softmax, flat_rows,
        utterances=utterances, frames=frames, pieces=pieces, vocabulary=vocabulary,
    )

    row_grad = lax.dot_general(
        logit_grad, out_weight, (((1,), (1,)), ((), ())), preferred_element_type=jnp.float32
    )
    row_grad = row_grad.astype(jnp.bfloat16).reshape(utterances, frames, depth)

    keep, send = cuts[:4], cuts[4:]
    block = depth // 2
    blocks = {k: keep[k] + partner(send[k], "seq", 1) for k in (2, 1, 3, 0)}
    total = blocks[0]
    for k in (2, 1, 3):
        total = total + crosswise(blocks[k], k, True)
    total, row_grad = lax.optimization_barrier((total, row_grad))
    block = block // 4
    blocks = [total[k * block : (k + 1) * block] for k in range(4)]
    total = blocks[0]
    for k in (2, 1, 3):
        total = total + crosswise(blocks[k], k, False)
    block = block // 4
    blocks = [total[k * block : (k + 1) * block] for k in range(4)]
    total = blocks[0]
    for k in (2, 1, 3):
        total = total + up_z(blocks[k], 2 * k)
    total = total + partner(total, "dp", 1)
    weight_grad = jnp.where(group % 2 == 0, total[:, : lanes // 2], total[:, lanes // 2 :])
    return (logit_grad.reshape(utterances, frames, vocabulary), row_grad, weight_grad)


def solution(mesh):
    placed = (P("dp", "seq", None), P(), P("dp", None), P("dp"), P("dp"))
    return jax.shard_map(
        shards,
        mesh=mesh,
        in_specs=placed,
        out_specs=(P("dp", "seq", None), P("dp", "seq", None), P("dp", "seq")),
        check_vma=False,
    )
```
